128 devices in a mesh: seq: 16 (over y, x_hi, core), head: 4 (over z), dp: 2 (over x_lo).
Axes of the slice: x: 4 (x_hi: 2, x_lo: 2; x = x_hi * 2 + x_lo), y: 4, z: 4, core: 2. Of those that a mesh axis runs over, the one named last changes fastest.
Arguments:
- inputs_x: bfloat16 [2, 16384, 8192], P('dp', 'seq', 'head'), may hold values from -6 to 6
- inputs_bc: bfloat16 [2, 16384, 256], P('dp', 'seq'), may hold values from -9 to 9
- dt_raw: float32 [2, 16384, 128], P('dp', 'seq', 'head'), may hold values from -14 to 0
- grad_out: bfloat16 [2, 16384, 8192], P('dp', 'seq', 'head'), may hold values from -12 to 12
- a_log: float32 [128], P('head'), may hold values from 0 to 0.7
- dt_bias: float32 [128], P('head'), may hold values from -0.3 to 0.3
- skip: float32 [128], P('head'), may hold values from 0.5 to 1.5
Outputs:
- grad_x: bfloat16 [2, 16384, 8192], P('dp', 'seq', 'head')
- grad_bc: float32 [2, 16384, 256], P('dp', 'seq')
- grad_dt: float32 [2, 16384, 128], P('dp', 'seq', 'head')
- grad_heads: float32 [3, 128], P(None, 'head')
The draws below stay inside these ranges and needn't reach their ends.
All inputs are finite; a program needn't handle non-finite values.
Results may differ from the reference program's by a relative error of at most 0.0014.
Values sent between devices are 32-bit elements; how exact they have to be, the bound alone decides.
A program may use at most 192 MiB of HBM per device.

```python
import math
import jax
import jax.numpy as jnp
from jax import lax

H = 128
P_SIZE = 64
N = 128
GROUP = 256
TOK_DEV = 1024
SEQLEN = 16384
SEQS = 2
INNER = 8192


def draw_dt_raw(key, part):
    key = jax.random.fold_in(key, 11)
    keys = jax.random.split(key, 6)
    quick = 5
    fast = jax.random.randint(keys[0], (H,), 0, 10) < quick
    tree_level = jnp.where(fast, -4.0, math.log(0.3 / SEQLEN)) + jax.random.uniform(keys[1], (H,), jnp.float32, -0.3, 0.3)
    shard_spans = jax.random.uniform(keys[2], (SEQS, SEQLEN // TOK_DEV, 1, H), jnp.float32, -0.35, 0.35)
    shard_spans = jnp.broadcast_to(shard_spans, (SEQS, SEQLEN // TOK_DEV, TOK_DEV, H)).reshape(SEQS, SEQLEN, H)
    noise_amount = jax.random.uniform(keys[3], (SEQS, SEQLEN, H), jnp.float32, -0.35, 0.35)
    token_spots = jax.random.randint(keys[4], (SEQS, 3), 0, SEQLEN)
    shard_places = jnp.arange(SEQLEN)
    shard_width = jnp.any(shard_places[None, :, None] == token_spots[:, None, :], axis=2)
    head_extent = jax.random.uniform(keys[5], (SEQS, SEQLEN, H), jnp.float32, -1.4, -0.9)
    return jnp.where(shard_width[:, :, None], head_extent, tree_level[None, None, :] + shard_spans + noise_amount)


def draw_grad_out(key, part):
    key = jax.random.fold_in(key, 23)
    first = jax.random.fold_in(key, 0)
    shard_places = jnp.arange(SEQLEN, dtype=jnp.float32) / SEQLEN
    ramp = 0.5 + shard_places
    values = jnp.clip(jax.random.normal(first, (SEQS, SEQLEN, INNER), jnp.float32), -4.0, 4.0)
    return (values * ramp[None, :, None]).astype(jnp.bfloat16)


def level_of(stream_key, shape, pieces, smallest, high):
    gain = 1.0
    for dim, blocks in pieces:
        steps = jax.random.uniform(jax.random.fold_in(jax.random.fold_in(stream_key, 6), dim), (blocks,), jnp.float32, smallest / len(pieces), high / len(pieces))
        gain = gain * jnp.repeat(jnp.exp(steps), shape[dim] // blocks).reshape((-1,) + (1,) * (len(shape) - 1 - dim))
    return gain


def gaussian(stream_key, dims, scale, limit, cuts=(), held_as=jnp.bfloat16):
    result = scale * jax.random.normal(stream_key, dims, jnp.float32)
    if cuts:
        result = result * level_of(stream_key, dims, cuts, -0.22, 0.18)
    return jnp.clip(result, -limit, limit).astype(held_as)


def setup_inputs(seed: int = 0) -> dict:
    seeds = jax.random.split(jax.random.key(seed), 8)
    return {
        "inputs_x": gaussian(seeds[0], (SEQS, SEQLEN, INNER), 1.0, 6.0, ((0, 2), (1, 16), (2, 4))),
        "inputs_bc": gaussian(seeds[1], (SEQS, SEQLEN, 2 * N), 1.5, 9.0, ((0, 2), (1, 16))),
        "dt_raw": draw_dt_raw(jax.random.fold_in(seeds[7], 71), 0),
        "grad_out": draw_grad_out(jax.random.fold_in(seeds[7], 71), 0),
        "a_log": jnp.clip(0.7 * jax.random.uniform(seeds[4], (H,), jnp.float32) ** level_of(seeds[4], (H,), ((0, 4),), -0.2, 0.2), 0.0, 0.7),
        "dt_bias": jnp.clip(jax.random.uniform(seeds[5], (H,), jnp.float32, -0.3, 0.3) * level_of(seeds[5], (H,), ((0, 4),), -0.4, 0.0), -0.3, 0.3),
        "skip": jnp.clip(1.0 + 0.1 * jax.random.normal(seeds[6], (H,), jnp.float32), 0.5, 1.5),
    }


HIGH = lax.Precision.HIGHEST

def block_grads(xf, yf, bmat, cmat, dtv, cum, hin, gout):
    size = cum.shape[0]
    lower = (jnp.arange(size)[:, None] >= jnp.arange(size)[None, :])[:, :, None]
    gap = cum[:, None, :] - cum[None, :, :]
    decay = jnp.where(lower, jnp.exp(jnp.where(lower, gap, 0.0)), 0.0)
    xs = xf * dtv[:, :, None]
    scores = jnp.dot(cmat, bmat.T, precision=HIGH)
    paired = jnp.einsum('ihp,jhp->ijh', yf, xs, precision=HIGH) * decay
    weight = scores[:, :, None] * decay
    wend = jnp.exp(cum[-1][None, :] - cum)
    spread = jnp.einsum('hpn,jn->jhp', gout, bmat, precision=HIGH)
    dxs = jnp.einsum('ijh,ihp->jhp', weight, yf, precision=HIGH) + wend[:, :, None] * spread
    summed = lax.optimization_barrier(jnp.sum(paired, axis=2))
    grad_b = jnp.dot(summed.T, cmat, precision=HIGH) + jnp.einsum('jhp,hpn->jn', xs * wend[:, :, None], gout, precision=HIGH)
    lifted = yf * jnp.exp(cum)[:, :, None]
    grad_c = jnp.dot(summed, bmat, precision=HIGH) + jnp.einsum('ihp,hpn->in', lifted, hin, precision=HIGH)
    inner = scores[:, :, None] * paired
    edge = wend * lax.optimization_barrier(jnp.sum(xs * spread, axis=2))
    carried = jnp.einsum('in,hpn->ihp', cmat, hin, precision=HIGH)
    dcum = lax.optimization_barrier(jnp.sum(inner, axis=1)) - lax.optimization_barrier(jnp.sum(inner, axis=0)) + lax.optimization_barrier(jnp.sum(lifted * carried, axis=2)) - edge
    closing = jnp.exp(cum[-1]) * lax.optimization_barrier(jnp.sum(gout * hin, axis=(1, 2))) + lax.optimization_barrier(jnp.sum(edge, axis=0))
    dcum = dcum.at[size - 1].add(closing)
    dlog = jnp.flip(jnp.cumsum(jnp.flip(dcum, 0), axis=0), 0)
    return (dxs, grad_b, grad_c, dlog, lifted)

def reference(inputs_x, inputs_bc, dt_raw, grad_out, a_log, dt_bias, skip):
    blocks = SEQLEN // GROUP
    rate = -jnp.exp(a_log)
    shifted = dt_raw + dt_bias[None, None, :]
    step_dt = jax.nn.softplus(shifted)
    cumul = jnp.cumsum((step_dt * rate[None, None, :]).reshape(SEQS, blocks, GROUP, H), axis=2)

    def split(array):
        return jnp.swapaxes(array.reshape((SEQS, blocks, GROUP) + array.shape[2:]), 0, 1)

    def join(array):
        return jnp.swapaxes(array, 0, 1).reshape((SEQS, SEQLEN) + array.shape[3:])
    x_blocks = split(inputs_x.reshape(SEQS, SEQLEN, H, P_SIZE))
    y_blocks = split(grad_out.reshape(SEQS, SEQLEN, H, P_SIZE))
    b_blocks = split(inputs_bc[:, :, :N].astype(jnp.float32))
    c_blocks = split(inputs_bc[:, :, N:].astype(jnp.float32))
    dt_blocks = split(step_dt)
    cum_blocks = jnp.swapaxes(cumul, 0, 1)

    def forward(carry, operands):
        x_blk, b_blk, dt_blk, cum_blk = operands
        xs = x_blk.astype(jnp.float32) * dt_blk[..., None]
        wend = jnp.exp(cum_blk[:, -1:, :] - cum_blk)
        fresh = jnp.einsum('sqhp,sqn->shpn', xs * wend[..., None], b_blk, precision=HIGH)
        return (jnp.exp(cum_blk[:, -1, :])[:, :, None, None] * carry + fresh, carry)
    zero = jnp.zeros((SEQS, H, P_SIZE, N), jnp.float32)
    _, entering = lax.scan(forward, zero, (x_blocks, b_blocks, dt_blocks, cum_blocks))
    batched = jax.vmap(block_grads)

    def backward(carry, operands):
        x_blk, y_blk, b_blk, c_blk, dt_blk, cum_blk, hin = operands
        dxs, grad_b, grad_c, dlog, lifted = batched(x_blk.astype(jnp.float32), y_blk.astype(jnp.float32), b_blk, c_blk, dt_blk, cum_blk, hin, carry)
        before = jnp.exp(cum_blk[:, -1, :])[:, :, None, None] * carry + jnp.einsum('sqhp,sqn->shpn', lifted, c_blk, precision=HIGH)
        return (before, (dxs, grad_b, grad_c, dlog))
    _, (dxs, grad_b, grad_c, dlog) = lax.scan(backward, zero, (x_blocks, y_blocks, b_blocks, c_blocks, dt_blocks, cum_blocks, entering), reverse=True)
    dxs = join(dxs)
    dlog = join(dlog)
    xf = inputs_x.reshape(SEQS, SEQLEN, H, P_SIZE).astype(jnp.float32)
    yf = grad_out.reshape(SEQS, SEQLEN, H, P_SIZE).astype(jnp.float32)
    grad_x = (dxs * step_dt[..., None] + skip[None, None, :, None] * yf).reshape(SEQS, SEQLEN, INNER).astype(jnp.bfloat16)
    grad_bc = jnp.concatenate([join(grad_b), join(grad_c)], axis=2)
    grad_dt = (lax.optimization_barrier(jnp.sum(dxs * xf, axis=3)) + dlog * rate[None, None, :]) * jax.nn.sigmoid(shifted)
    scale = 1.0 / math.sqrt(SEQS * SEQLEN)
    d_alog = lax.optimization_barrier(jnp.sum(dlog * step_dt, axis=(0, 1))) * rate
    d_bias = lax.optimization_barrier(jnp.sum(grad_dt, axis=(0, 1)))
    d_skip = lax.optimization_barrier(jnp.sum(yf * xf, axis=(0, 1, 3)))
    grad_heads = jnp.stack([d_alog, d_bias, d_skip]) * scale
    return (grad_x, grad_bc, grad_dt, grad_heads)
```

```python
import functools
import math

import jax
import jax.numpy as jnp
from jax import lax
from jax.experimental import pallas as pl
from jax.experimental.pallas import tpu as pltpu
from jax.sharding import PartitionSpec as P

Q = 64
CHUNK = 256
HEADDIM = 64
LANES = 128
HIGH = lax.Precision.HIGHEST
F32 = jnp.float32
BF16 = jnp.bfloat16
VMEM_LIMIT = 56 * 1024 * 1024


def dot_nn(a, b, precision=None):
    return lax.dot_general(a, b, (((1,), (0,)), ((), ())), precision=precision, preferred_element_type=F32)


def dot_nt(a, b):
    return lax.dot_general(a, b, (((1,), (1,)), ((), ())), preferred_element_type=F32)


def halves(value):
    hi = value.astype(BF16)
    return hi, (value - hi.astype(F32)).astype(BF16)


def iota(shape, dim):
    return lax.broadcasted_iota(jnp.int32, shape, dim)


def triangle(upper):
    r, c = iota((Q, Q), 0), iota((Q, Q), 1)
    return jnp.where(r <= c if upper else r >= c, 1.0, 0.0).astype(F32)


def repeat_heads(value, heads):
    pick = jnp.where(iota((heads, LANES), 1) % heads == iota((heads, LANES), 0), 1.0, 0.0)
    return dot_nn(value, pick.astype(F32), HIGH)


def packed(value, heads, terms):
    lane = iota(value.shape, 1)
    total = jnp.zeros_like(value)
    rest = value
    for term in range(terms):
        part = rest.astype(BF16).astype(F32)
        total = jnp.where((lane >= term * heads) & (lane < (term + 1) * heads), part, total)
        rest = rest - part
    return total.astype(BF16)


def head_lanes(heads, width):
    shape = (LANES, width)
    return jnp.where(iota(shape, 0) % heads == iota(shape, 1) // HEADDIM, 1.0, 0.0).astype(BF16)


def edges_kernel(heads, x_ref, y_ref, bc_ref, dt_ref, bias_ref, alog_ref, ends_ref, starts_ref, decay_ref,
                 pe, pf, bt, ct, sel, xs, ys, dec):
    length = dt_ref.shape[0]
    blocks = length // Q
    step = pl.program_id(0)

    @pl.when(step == 0)
    def _():
        sel[...] = head_lanes(heads, sel.shape[1])
        rate = -jnp.exp(repeat_heads(jnp.broadcast_to(alog_ref[...], (8, heads)), heads))[:1]
        dt = jax.nn.softplus(repeat_heads(dt_ref[...] + bias_ref[...], heads))
        tri = triangle(False)
        cums = [dot_nn(tri, dt[k * Q:(k + 1) * Q] * rate, HIGH) for k in range(blocks)]
        before = jnp.zeros((1, LANES), F32)
        for k in range(blocks):
            pe[pl.ds(k * Q, Q), :] = packed(jnp.exp(cums[k] + before), heads, 2)
            before = before + cums[k][Q - 1:Q]
        after = jnp.zeros((1, LANES), F32)
        for k in reversed(range(blocks)):
            last = cums[k][Q - 1:Q]
            pf[pl.ds(k * Q, Q), :] = packed(dt[k * Q:(k + 1) * Q] * jnp.exp((last - cums[k]) + after), heads, 2)
            after = after + last
        dec[...] = packed(jnp.broadcast_to(jnp.exp(before), (8, LANES)), heads, 3)
        b_t = jnp.transpose(bc_ref[:, :LANES].astype(F32)).astype(BF16)
        c_t = jnp.transpose(bc_ref[:, LANES:].astype(F32)).astype(BF16)
        bt[:, :length] = b_t
        bt[:, length:] = b_t
        ct[:, :length] = c_t
        ct[:, length:] = c_t

    here = sel[:, pl.ds(pl.multiple_of(step * CHUNK, CHUNK), CHUNK)]
    hi, lo = halves(dot_nn(pf[...], here) * x_ref[...].astype(F32))
    xs[:length] = hi
    xs[length:] = lo
    ends_ref[...] = dot_nn(bt[...], xs[...])
    hi, lo = halves(dot_nn(pe[...], here) * y_ref[...].astype(F32))
    ys[:length] = hi
    ys[length:] = lo
    starts_ref[...] = dot_nn(ct[...], ys[...])
    decay_ref[...] = dot_nn(dec[...], here)


def edges(x, y, bc, dt, bias, alog):
    length, width = x.shape
    heads = dt.shape[1]
    state = bc.shape[1] // 2
    whole = pl.BlockSpec(memory_space=pltpu.VMEM)
    piece = lambda rows: pl.BlockSpec((rows, CHUNK), lambda i: (0, i))
    return pl.pallas_call(
        functools.partial(edges_kernel, heads),
        grid=(width // CHUNK,),
        out_shape=(
            jax.ShapeDtypeStruct((state, width), F32),
            jax.ShapeDtypeStruct((state, width), F32),
            jax.ShapeDtypeStruct((8, width), F32),
        ),
        in_specs=[piece(length), piece(length), whole, whole, whole, whole],
        out_specs=(piece(state), piece(state), piece(8)),
        scratch_shapes=[
            pltpu.VMEM((length, LANES), BF16),
            pltpu.VMEM((length, LANES), BF16),
            pltpu.VMEM((state, 2 * length), BF16),
            pltpu.VMEM((state, 2 * length), BF16),
            pltpu.VMEM((LANES, width), BF16),
            pltpu.VMEM((2 * length, CHUNK), BF16),
            pltpu.VMEM((2 * length, CHUNK), BF16),
            pltpu.VMEM((8, LANES), BF16),
        ],
        compiler_params=pltpu.CompilerParams(vmem_limit_bytes=VMEM_LIMIT, dimension_semantics=("arbitrary",)),
        cost_estimate=pl.CostEstimate(flops=8 * length * width * state, bytes_accessed=4 * length * width, transcendentals=0),
    )(x, y, bc, dt, bias, alog)


def main_kernel(heads, xf_ref, yf_ref, xb_ref, yb_ref, bc_ref, dt_ref, bias_ref, alog_ref, skip_ref, hin_ref, gin_ref,
                gx_ref, gbc_ref, gdt_ref, gheads_ref,
                pe, pf, dts, shs, sel, rows, vs, ws, zf, zb, ll, xx, prods, hst, gst, yx):
    length = dt_ref.shape[0]
    width = sel.shape[1]
    blocks = length // Q
    step = pl.program_id(0)
    kf = step
    kb = blocks - 1 - step
    chunks = [slice(c * CHUNK, (c + 1) * CHUNK) for c in range(width // CHUNK)]
    rate = -jnp.exp(repeat_heads(jnp.broadcast_to(alog_ref[...], (8, heads)), heads))[:1]

    @pl.when(step == 0)
    def _():
        sel[...] = head_lanes(heads, width)
        shifted = repeat_heads(dt_ref[...] + bias_ref[...], heads)
        shs[...] = shifted
        dt = jax.nn.softplus(shifted)
        dts[...] = dt
        tri = triangle(False)
        mids, lasts = [], []
        for k in range(blocks):
            here = dt[k * Q:(k + 1) * Q]
            cum = dot_nn(tri, here * rate, HIGH)
            mid = cum[Q // 2 - 1:Q // 2]
            pe[pl.ds(k * Q, Q), :] = packed(jnp.exp(cum - mid), heads, 2)
            pf[pl.ds(k * Q, Q), :] = packed(here * jnp.exp(mid - cum), heads, 2)
            mids.append(mid)
            lasts.append(cum[Q - 1:Q])
        for k in range(blocks):
            gone = jnp.broadcast_to(jnp.exp(lasts[k] - mids[k]), (8, LANES))
            come = jnp.broadcast_to(jnp.exp(mids[k]), (8, LANES))
            factor = packed(jnp.where(iota((8, LANES), 0) == 0, gone, come), heads, 3)
            rows[k] = dot_nn(factor, sel[...])
        skips = repeat_heads(jnp.broadcast_to(skip_ref[...], (8, heads)), heads)
        rows[blocks] = dot_nn(packed(skips, heads, 3), sel[...])
        yx[...] = jnp.zeros_like(yx)
        gbc_ref[...] = jnp.zeros_like(gbc_ref)
        for c in chunks:
            h = hin_ref[:, c] * rows[0, 1:2, c]
            hst[:, c] = h
            zf[0:128, c], zf[256:384, c] = halves(h)
            g = gin_ref[:, c] * rows[blocks - 1, 0:1, c]
            gst[:, c] = g
            zb[0:128, c], zb[256:384, c] = halves(g)

    spanf = pl.ds(pl.multiple_of(kf * Q, Q), Q)
    spanb = pl.ds(pl.multiple_of(kb * Q, Q), Q)
    lane = iota((Q, 2 * Q), 1)
    row = iota((Q, 2 * Q), 0)

    b_f, c_f = bc_ref[spanf, :LANES], bc_ref[spanf, LANES:]
    b_b, c_b = bc_ref[spanb, :LANES], bc_ref[spanb, LANES:]
    b_ff = jnp.concatenate([b_f, b_f], axis=0)
    c_bb = jnp.concatenate([c_b, c_b], axis=0)
    zero = jnp.zeros((Q, 2 * Q), F32)

    lower = row >= lane % Q
    s_hi, s_lo = halves(jnp.where(lower, dot_nt(c_f, b_ff), zero))
    first_f = jnp.concatenate([c_f, s_hi], axis=1)
    second_f = jnp.concatenate([s_lo, c_f], axis=1)
    upper = row <= lane % Q
    s_hi, s_lo = halves(jnp.where(upper, dot_nt(b_b, c_bb), zero))
    first_b = jnp.concatenate([b_b, s_hi], axis=1)
    second_b = jnp.concatenate([s_lo, b_b], axis=1)

    for c in chunks:
        e = dot_nn(pe[spanf, :], sel[:, c])
        f = dot_nn(pf[spanf, :], sel[:, c])
        lifted = e * yf_ref[:, c].astype(F32)
        xs = f * xf_ref[:, c].astype(F32)
        zf[192:256, c], zf[128:192, c] = halves(xs)
        ll[0:64, c], ll[64:128, c] = halves(lifted)
        out = dot_nn(first_f, zf[0:256, c]) + dot_nn(second_f, zf[128:384, c])
        prods[0:64, c], prods[64:128, c] = halves(lifted * out)

        e = dot_nn(pe[spanb, :], sel[:, c])
        f = dot_nn(pf[spanb, :], sel[:, c])
        y = yb_ref[:, c].astype(F32)
        x = xb_ref[:, c].astype(F32)
        lifted = e * y
        xs = f * x
        zb[192:256, c], zb[128:192, c] = halves(lifted)
        xx[0:64, c], xx[64:128, c] = halves(xs)
        out = dot_nn(first_b, zb[0:256, c]) + dot_nn(second_b, zb[128:384, c])
        prods[128:192, c], prods[192:256, c] = halves(xs * out)
        gx_ref[:, c] = (f * out + rows[blocks, :1, c] * y).astype(BF16)
        yx[:, c] += jnp.sum((y * x).reshape(Q // 8, 8, CHUNK), axis=0)

    sums = dot_nt(prods[...], sel[...])
    vs[spanf, :] = sums[0:64] + sums[64:128]
    ws[spanb, :] = sums[128:192] + sums[192:256]

    r1 = dot_nt(ll[...], zf[0:256, :])
    r2 = dot_nt(ll[0:64, :], zf[256:384, :])
    pair = r1[:64, 128:] + r1[64:, 128:]
    pair = jnp.where(lower, pair, zero)
    p_hi, p_lo = halves(pair)
    grad_c = r1[:64, :128] + r1[64:, :128] + r2 + dot_nn(p_hi, b_ff) + dot_nn(p_lo, b_ff)
    turned = jnp.transpose(pair)
    t_hi, t_lo = halves(turned[:64] + turned[64:])
    gbc_ref[spanf, LANES:] = grad_c
    gbc_ref[spanf, :LANES] += dot_nn(t_hi, c_f) + dot_nn(t_lo, c_f)
    r1 = dot_nt(xx[...], zb[0:128, :])
    r2 = dot_nt(xx[0:64, :], zb[256:384, :])
    gbc_ref[spanb, :LANES] += r1[:64] + r1[64:] + r2

    bt = jnp.transpose(b_ff.astype(F32)).astype(BF16)
    ct = jnp.transpose(c_bb.astype(F32)).astype(BF16)
    last = step == blocks - 1
    for c in chunks:
        come = jnp.where(last, 1.0, rows[jnp.minimum(kf + 1, blocks - 1), 1:2, c])
        h = (hst[:, c] + dot_nn(bt, zf[128:256, c])) * rows[kf, 0:1, c] * come
        hst[:, c] = h
        zf[0:128, c], zf[256:384, c] = halves(h)
        g = (gst[:, c] + dot_nn(ct, zb[128:256, c])) * rows[kb, 1:2, c] * rows[jnp.maximum(kb - 1, 0), 0:1, c]
        gst[:, c] = g
        zb[0:128, c], zb[256:384, c] = halves(g)

    @pl.when(step == blocks - 1)
    def _():
        closing = jnp.sum(gin_ref[...] * hst[...], axis=0, keepdims=True)
        totals = jnp.concatenate([closing, jnp.sum(yx[...], axis=0, keepdims=True), jnp.zeros((14, width), F32)], axis=0)
        hi, lo = halves(totals)
        totals = dot_nt(hi, sel[...]) + dot_nt(lo, sel[...])
        after = totals[0:1]
        tri = triangle(True)
        d_alog = jnp.zeros((1, LANES), F32)
        d_bias = jnp.zeros((1, LANES), F32)
        for k in reversed(range(blocks)):
            span = slice(k * Q, (k + 1) * Q)
            w = ws[span]
            dt = dts[span]
            dlog = dot_nn(tri, vs[span] - w, HIGH) + after
            after = dlog[0:1]
            grad_dt = (w / dt + dlog * rate) * jax.nn.sigmoid(shs[span])
            gdt_ref[span, :] = grad_dt[:, :heads]
            d_alog = d_alog + jnp.sum(dlog * dt, axis=0, keepdims=True)
            d_bias = d_bias + jnp.sum(grad_dt, axis=0, keepdims=True)
        gheads_ref[...] = jnp.concatenate(
            [d_alog * rate, d_bias, totals[1:2], jnp.zeros((5, LANES), F32)], axis=0)


def main(x, y, bc, dt, bias, alog, skip, hin, gin):
    length, width = x.shape
    heads = dt.shape[1]
    state = bc.shape[1] // 2
    blocks = length // Q
    whole = pl.BlockSpec(memory_space=pltpu.VMEM)
    ahead = pl.BlockSpec((Q, width), lambda i: (i, 0))
    back = pl.BlockSpec((Q, width), lambda i: (blocks - 1 - i, 0))
    return pl.pallas_call(
        functools.partial(main_kernel, heads),
        grid=(blocks,),
        out_shape=(
            jax.ShapeDtypeStruct((length, width), BF16),
            jax.ShapeDtypeStruct((length, 2 * state), F32),
            jax.ShapeDtypeStruct((length, heads), F32),
            jax.ShapeDtypeStruct((8, LANES), F32),
        ),
        in_specs=[ahead, ahead, back, back] + [whole] * 7,
        out_specs=(back, whole, whole, whole),
        scratch_shapes=[
            pltpu.VMEM((length, LANES), BF16),
            pltpu.VMEM((length, LANES), BF16),
            pltpu.VMEM((length, LANES), F32),
            pltpu.VMEM((length, LANES), F32),
            pltpu.VMEM((LANES, width), BF16),
            pltpu.VMEM((blocks + 1, 8, width), F32),
            pltpu.VMEM((length, LANES), F32),
            pltpu.VMEM((length, LANES), F32),
            pltpu.VMEM((384, width), BF16),
            pltpu.VMEM((384, width), BF16),
            pltpu.VMEM((128, width), BF16),
            pltpu.VMEM((128, width), BF16),
            pltpu.VMEM((256, width), BF16),
            pltpu.VMEM((state, width), F32),
            pltpu.VMEM((state, width), F32),
            pltpu.VMEM((8, width), F32),
        ],
        compiler_params=pltpu.CompilerParams(vmem_limit_bytes=VMEM_LIMIT, dimension_semantics=("arbitrary",)),
        cost_estimate=pl.CostEstimate(flops=60 * length * width * state, bytes_accessed=12 * length * width, transcendentals=0),
    )(x, y, x, y, bc, dt, bias, alog, skip, hin, gin)


def carried_in(decay, value, axis, reverse):
    count, place = (lax.axis_size(axis), lax.axis_index(axis))
    decays = lax.all_gather(decay, axis)
    values = lax.all_gather(value, axis)

    def hop(k, before):
        at = count - 1 - k if reverse else k
        reached = at > place if reverse else at < place
        return jnp.where(reached, decays[at] * before + values[at], before)

    return lax.fori_loop(0, count, hop, jnp.zeros_like(value))


def shards(inputs_x, inputs_bc, dt_raw, grad_out, a_log, dt_bias, skip):
    length = inputs_x.shape[1]
    heads = a_log.shape[0]
    x, y, bc, dt = inputs_x[0], grad_out[0], inputs_bc[0], dt_raw[0]
    bias, alog, skips = dt_bias[None], a_log[None], skip[None]
    ends, starts, decay = edges(x, y, bc, dt, bias, alog)
    hin = carried_in(decay[:1], ends, "seq", False)
    gin = carried_in(decay[:1], starts, "seq", True)
    grad_x, grad_bc, grad_dt, sums = main(x, y, bc, dt, bias, alog, skips, hin, gin)
    grad_bc = lax.psum(grad_bc, "head")
    sequences = inputs_x.shape[0] * lax.axis_size("dp")
    scale = 1.0 / math.sqrt(sequences * length * lax.axis_size("seq"))
    grad_heads = lax.psum(sums[:3, :heads], ("seq", "dp")) * scale
    return (grad_x[None], grad_bc[None], grad_dt[None], grad_heads)


def solution(mesh):
    placed = (
        P("dp", "seq", "head"),
        P("dp", "seq", None),
        P("dp", "seq", "head"),
        P("dp", "seq", "head"),
        P("head"),
        P("head"),
        P("head"),
    )
    return jax.shard_map(
        shards,
        mesh=mesh,
        in_specs=placed,
        out_specs=(
            P("dp", "seq", "head"),
            P("dp", "seq", None),
            P("dp", "seq", "head"),
            P(None, "head"),
        ),
        check_vma=False,
    )
```

```python
import functools
import math

import jax
import jax.numpy as jnp
from jax import lax
from jax.experimental import pallas as pl
from jax.experimental.pallas import tpu as pltpu
from jax.sharding import PartitionSpec as P

Q = 64
CHUNK = 256
HEADDIM = 64
LANES = 128
HIGH = lax.Precision.HIGHEST
F32 = jnp.float32
BF16 = jnp.bfloat16
VMEM_LIMIT = 56 * 1024 * 1024


def dot_nn(a, b, precision=None):
    return lax.dot_general(a, b, (((1,), (0,)), ((), ())), precision=precision, preferred_element_type=F32)


def dot_nt(a, b):
    return lax.dot_general(a, b, (((1,), (1,)), ((), ())), preferred_element_type=F32)


def halves(value):
    hi = value.astype(BF16)
    return hi, (value - hi.astype(F32)).astype(BF16)


def iota(shape, dim):
    return lax.broadcasted_iota(jnp.int32, shape, dim)


def triangle(upper):
    r, c = iota((Q, Q), 0), iota((Q, Q), 1)
    return jnp.where(r <= c if upper else r >= c, 1.0, 0.0).astype(F32)


def repeat_heads(value, heads):
    pick = jnp.where(iota((heads, LANES), 1) % heads == iota((heads, LANES), 0), 1.0, 0.0)
    return dot_nn(value, pick.astype(F32), HIGH)


def packed(value, heads, terms):
    lane = iota(value.shape, 1)
    total = jnp.zeros_like(value)
    rest = value
    for term in range(terms):
        part = rest.astype(BF16).astype(F32)
        total = jnp.where((lane >= term * heads) & (lane < (term + 1) * heads), part, total)
        rest = rest - part
    return total.astype(BF16)


def head_lanes(heads, width):
    shape = (LANES, width)
    return jnp.where(iota(shape, 0) % heads == iota(shape, 1) // HEADDIM, 1.0, 0.0).astype(BF16)


def steps_of(dt_ref, bias_ref, heads):
    turned = jnp.transpose(jnp.concatenate([dt_ref[...]] * (LANES // heads), axis=0))
    return turned + repeat_heads(jnp.broadcast_to(bias_ref[...], (8, heads)), heads)[:1]


def rates_of(alog_ref, heads):
    return -jnp.exp(repeat_heads(jnp.broadcast_to(alog_ref[...], (8, heads)), heads))[:1]


def edges_kernel(heads, x_ref, y_ref, bc_ref, dt_ref, bias_ref, alog_ref, hin_ref, gin_ref,
                 pe, pf, bt, ct, sel, xb, yb, xs, ys, dec, mine, out0, got0, chip, gath, pre, inc, fin,
                 load_sem, s0, r0, s1, r1, s2, r2, s3, r3):
    length = bc_ref.shape[0]
    blocks = length // Q
    groups = hin_ref.shape[0]
    state = hin_ref.shape[1]
    me = lax.axis_index("seq")
    core = lax.rem(me, 2)
    place = me // 2
    ahead = core == 1
    partner = me + 1 - 2 * core

    def peer(d):
        return lax.rem(place + d, groups)

    def loads(i):
        g = peer(1 + i)
        span = pl.ds(pl.multiple_of(g * CHUNK, CHUNK), CHUNK)
        return (pltpu.make_async_copy(x_ref.at[:, span], xb.at[i], load_sem.at[0, i]),
                pltpu.make_async_copy(y_ref.at[:, span], yb.at[i], load_sem.at[1, i]))

    def swap(i):
        return pltpu.make_async_remote_copy(
            src_ref=out0.at[i], dst_ref=got0.at[i], send_sem=s0.at[i], recv_sem=r0.at[i],
            device_id={"seq": partner}, device_id_type=pl.DeviceIdType.MESH)

    def spread(d):
        return pltpu.make_async_remote_copy(
            src_ref=chip.at[d - 1], dst_ref=gath.at[place], send_sem=s1.at[d - 1], recv_sem=r1.at[place],
            device_id={"seq": peer(d) * 2 + core}, device_id_type=pl.DeviceIdType.MESH)

    def spread_in(source):
        return pltpu.make_async_remote_copy(
            src_ref=chip.at[0], dst_ref=gath.at[source], send_sem=s1.at[0], recv_sem=r1.at[source],
            device_id={"seq": source * 2 + core}, device_id_type=pl.DeviceIdType.MESH)

    def back(pos):
        return pltpu.make_async_remote_copy(
            src_ref=pre.at[pos], dst_ref=inc.at[place], send_sem=s2.at[pos], recv_sem=r2.at[place],
            device_id={"seq": pos * 2 + core}, device_id_type=pl.DeviceIdType.MESH)

    def back_in(source):
        return pltpu.make_async_remote_copy(
            src_ref=pre.at[source], dst_ref=inc.at[source], send_sem=s2.at[source], recv_sem=r2.at[source],
            device_id={"seq": source * 2 + core}, device_id_type=pl.DeviceIdType.MESH)

    def hand(g):
        return pltpu.make_async_remote_copy(
            src_ref=inc.at[g], dst_ref=fin.at[g], send_sem=s3.at[g], recv_sem=r3.at[g],
            device_id={"seq": partner}, device_id_type=pl.DeviceIdType.MESH)

    for i in range(groups):
        for copy in loads(i):
            copy.start()
    barrier = pltpu.get_barrier_semaphore()
    pl.semaphore_signal(barrier, inc=1, device_id={"seq": partner}, device_id_type=pl.DeviceIdType.MESH)
    for d in range(1, groups):
        pl.semaphore_signal(barrier, inc=1, device_id={"seq": peer(d) * 2 + core}, device_id_type=pl.DeviceIdType.MESH)

    sel[...] = head_lanes(heads, sel.shape[1])
    rate = rates_of(alog_ref, heads)
    dt = jax.nn.softplus(steps_of(dt_ref, bias_ref, heads))
    tri = triangle(False)
    cums = [dot_nn(tri, dt[k * Q:(k + 1) * Q] * rate, HIGH) for k in range(blocks)]
    before = jnp.zeros((1, LANES), F32)
    for k in range(blocks):
        pe[pl.ds(k * Q, Q), :] = packed(jnp.exp(cums[k] + before), heads, 2)
        before = before + cums[k][Q - 1:Q]
    after = jnp.zeros((1, LANES), F32)
    for k in reversed(range(blocks)):
        last = cums[k][Q - 1:Q]
        pf[pl.ds(k * Q, Q), :] = packed(dt[k * Q:(k + 1) * Q] * jnp.exp((last - cums[k]) + after), heads, 2)
        after = after + last
    dec[...] = packed(jnp.broadcast_to(jnp.exp(before), (8, LANES)), heads, 3)
    b_t = jnp.transpose(bc_ref[:, :LANES].astype(F32)).astype(BF16)
    c_t = jnp.transpose(bc_ref[:, LANES:].astype(F32)).astype(BF16)
    bt[:, :length] = b_t
    bt[:, length:] = b_t
    ct[:, :length] = c_t
    ct[:, length:] = c_t
    pl.semaphore_wait(barrier, groups)

    def combine(i):
        swap(i).wait_recv()
        keep = out0[i, state:state + 1, :]
        value = mine[i] + keep * got0[i, :state, :]
        decay = out0[i, state:, :] * got0[i, state:, :]
        if i < groups - 1:
            chip[i, :state, :] = value
            chip[i, state:, :] = decay
            spread(i + 1).start()
        else:
            gath[place, :state, :] = value
            gath[place, state:, :] = decay

    for i in range(groups):
        g = peer(1 + i)
        here = sel[:, pl.ds(pl.multiple_of(g * CHUNK, CHUNK), CHUNK)]
        copy_x, copy_y = loads(i)
        copy_x.wait()
        hi, lo = halves(dot_nn(pf[...], here) * xb[i].astype(F32))
        xs[:length] = hi
        xs[length:] = lo
        ends = dot_nn(bt[...], xs[...])
        copy_y.wait()
        hi, lo = halves(dot_nn(pe[...], here) * yb[i].astype(F32))
        ys[:length] = hi
        ys[length:] = lo
        starts = dot_nn(ct[...], ys[...])
        mine[i] = jnp.where(ahead, ends, starts)
        out0[i, :state, :] = jnp.where(ahead, starts, ends)
        out0[i, state:, :] = dot_nn(dec[...], here)
        swap(i).start()
        if i:
            combine(i - 1)
    combine(groups - 1)

    total = jnp.zeros((state, CHUNK), F32)
    for d in range(1, groups):
        spread_in(peer(d)).wait_recv()
    for k in range(groups):
        pos = jnp.where(ahead, k, groups - 1 - k)

        @pl.when(pos == place)
        def _():
            inc[place] = total

        @pl.when(pos != place)
        def _():
            pre[pos] = total
            back(pos).start()

        total = gath[pos, state:state + 1, :] * total + gath[pos, :state, :]

    for d in range(groups):
        g = peer(d)
        if d:
            back_in(g).wait_recv()
        hand(g).start()
    for d in range(groups):
        g = peer(d)
        i = (d - 1) % groups
        own = got0[i, state:state + 1, :] * inc[g] + got0[i, :state, :]
        hand(g).wait_recv()
        other = fin[g]
        hin_ref[g] = jnp.where(ahead, own, other)
        gin_ref[g] = jnp.where(ahead, other, own)
    for i in range(groups):
        swap(i).wait_send()
        hand(i).wait_send()
    for d in range(1, groups):
        spread(d).wait_send()
        back(peer(d)).wait_send()


def edges(x, y, bc, dt, bias, alog):
    length, width = x.shape
    heads = dt.shape[0]
    state = bc.shape[1] // 2
    groups = width // CHUNK
    whole = pl.BlockSpec(memory_space=pltpu.VMEM)
    anywhere = pl.BlockSpec(memory_space=pl.ANY)
    dma = pltpu.SemaphoreType.DMA
    return pl.pallas_call(
        functools.partial(edges_kernel, heads),
        out_shape=(
            jax.ShapeDtypeStruct((groups, state, CHUNK), F32),
            jax.ShapeDtypeStruct((groups, state, CHUNK), F32),
        ),
        in_specs=[anywhere, anywhere, whole, whole, whole, whole],
        out_specs=(whole, whole),
        scratch_shapes=[
            pltpu.VMEM((length, LANES), BF16),
            pltpu.VMEM((length, LANES), BF16),
            pltpu.VMEM((state, 2 * length), BF16),
            pltpu.VMEM((state, 2 * length), BF16),
            pltpu.VMEM((LANES, width), BF16),
            pltpu.VMEM((groups, length, CHUNK), BF16),
            pltpu.VMEM((groups, length, CHUNK), BF16),
            pltpu.VMEM((2 * length, CHUNK), BF16),
            pltpu.VMEM((2 * length, CHUNK), BF16),
            pltpu.VMEM((8, LANES), BF16),
            pltpu.VMEM((groups, state, CHUNK), F32),
            pltpu.VMEM((groups, state + 8, CHUNK), F32),
            pltpu.VMEM((groups, state + 8, CHUNK), F32),
            pltpu.VMEM((groups - 1, state + 8, CHUNK), F32),
            pltpu.VMEM((groups, state + 8, CHUNK), F32),
            pltpu.VMEM((groups, state, CHUNK), F32),
            pltpu.VMEM((groups, state, CHUNK), F32),
            pltpu.VMEM((groups, state, CHUNK), F32),
            dma((2, groups)),
            dma((groups,)), dma((groups,)),
            dma((groups,)), dma((groups,)),
            dma((groups,)), dma((groups,)),
            dma((groups,)), dma((groups,)),
        ],
        compiler_params=pltpu.CompilerParams(vmem_limit_bytes=VMEM_LIMIT, collective_id=0, has_side_effects=True),
        cost_estimate=pl.CostEstimate(flops=8 * length * width * state, bytes_accessed=4 * length * width, transcendentals=0),
    )(x, y, bc, dt, bias, alog)


def main_kernel(heads, zs, dps, flats, scale, xf_ref, yf_ref, xb_ref, yb_ref, bc_ref, dt_ref, bias_ref, alog_ref, skip_ref, hin_ref, gin_ref,
                gx_ref, gbc_ref, gdt_ref, gheads_ref,
                pe, pf, dts, shs, sel, rows, vs, ws, zf, zb, ll, xx, prods, hst, gst, yx,
                part, stage, landed, done, hsum, hgot, s1, r1s, s2, r2s, s3, r3s):
    length = dts.shape[0]
    width = sel.shape[1]
    blocks = length // Q
    step = pl.program_id(0)
    kf = step
    kb = blocks - 1 - step
    chunks = [slice(c * CHUNK, (c + 1) * CHUNK) for c in range(width // CHUNK)]
    rate = rates_of(alog_ref, heads)
    half = blocks // 2
    lines = Q // zs
    z = lax.axis_index("head")
    flat = lax.axis_index("seq") * dps + lax.axis_index("dp")
    barrier = pltpu.get_barrier_semaphore()

    def zpeer(d):
        return {"head": lax.rem(z + d, zs)}

    def fpeer(d):
        other = lax.rem(flat + d, flats)
        return {"seq": other // dps, "dp": lax.rem(other, dps)}

    def scatter(j, d):
        q = lax.rem(z + d, zs)
        return pltpu.make_async_remote_copy(
            src_ref=stage.at[j, q], dst_ref=landed.at[j, z], send_sem=s1.at[j, q], recv_sem=r1s.at[j, z],
            device_id=zpeer(d), device_id_type=pl.DeviceIdType.MESH)

    def scatter_in(j, d):
        q = lax.rem(z + d, zs)
        return pltpu.make_async_remote_copy(
            src_ref=stage.at[j, q], dst_ref=landed.at[j, q], send_sem=s1.at[j, q], recv_sem=r1s.at[j, q],
            device_id=zpeer(d), device_id_type=pl.DeviceIdType.MESH)

    def gather(j, d):
        q = lax.rem(z + d, zs)
        return pltpu.make_async_remote_copy(
            src_ref=done.at[j, z], dst_ref=done.at[j, z], send_sem=s2.at[j, q], recv_sem=r2s.at[j, z],
            device_id=zpeer(d), device_id_type=pl.DeviceIdType.MESH)

    def gather_in(j, d):
        q = lax.rem(z + d, zs)
        return pltpu.make_async_remote_copy(
            src_ref=done.at[j, q], dst_ref=done.at[j, q], send_sem=s2.at[j, q], recv_sem=r2s.at[j, q],
            device_id=zpeer(d), device_id_type=pl.DeviceIdType.MESH)

    def share(d):
        return pltpu.make_async_remote_copy(
            src_ref=hsum, dst_ref=hgot.at[flat], send_sem=s3.at[d], recv_sem=r3s.at[flat],
            device_id=fpeer(d), device_id_type=pl.DeviceIdType.MESH)

    def share_in(d):
        other = lax.rem(flat + d, flats)
        return pltpu.make_async_remote_copy(
            src_ref=hsum, dst_ref=hgot.at[other], send_sem=s3.at[d], recv_sem=r3s.at[other],
            device_id=fpeer(d), device_id_type=pl.DeviceIdType.MESH)

    def reduce_pair(j):
        for d in range(1, zs):
            scatter_in(j, d).wait_recv()
        landed[j, z] = stage[j, z]
        total = landed[j, 0]
        for q in range(1, zs):
            total = total + landed[j, q]
        done[j, z] = total
        for d in range(1, zs):
            gather(j, d).start()

    def finish_pair(j):
        for d in range(1, zs):
            gather_in(j, d).wait_recv()
        for q in range(zs):
            gbc_ref[pl.ds(pl.multiple_of((half + j) * Q + q * lines, lines), lines), :] = done[j, q, :lines]
            gbc_ref[pl.ds(pl.multiple_of((half - 1 - j) * Q + q * lines, lines), lines), :] = done[j, q, lines:]

    @pl.when(step == 0)
    def _():
        for d in range(1, zs):
            pl.semaphore_signal(barrier, inc=1, device_id=zpeer(d), device_id_type=pl.DeviceIdType.MESH)

        @pl.loop(1, flats)
        def _(d):
            pl.semaphore_signal(barrier, inc=1, device_id=fpeer(d), device_id_type=pl.DeviceIdType.MESH)

        sel[...] = head_lanes(heads, width)
        shifted = steps_of(dt_ref, bias_ref, heads)
        shs[...] = shifted
        dt = jax.nn.softplus(shifted)
        dts[...] = dt
        tri = triangle(False)
        mids, lasts = [], []
        for k in range(blocks):
            here = dt[k * Q:(k + 1) * Q]
            cum = dot_nn(tri, here * rate, HIGH)
            mid = cum[Q // 2 - 1:Q // 2]
            pe[pl.ds(k * Q, Q), :] = packed(jnp.exp(cum - mid), heads, 2)
            pf[pl.ds(k * Q, Q), :] = packed(here * jnp.exp(mid - cum), heads, 2)
            mids.append(mid)
            lasts.append(cum[Q - 1:Q])
        for k in range(blocks):
            gone = jnp.broadcast_to(jnp.exp(lasts[k] - mids[k]), (8, LANES))
            come = jnp.broadcast_to(jnp.exp(mids[k]), (8, LANES))
            factor = packed(jnp.where(iota((8, LANES), 0) == 0, gone, come), heads, 3)
            rows[k] = dot_nn(factor, sel[...])
        skips = repeat_heads(jnp.broadcast_to(skip_ref[...], (8, heads)), heads)
        rows[blocks] = dot_nn(packed(skips, heads, 3), sel[...])
        yx[...] = jnp.zeros_like(yx)
        part[...] = jnp.zeros_like(part)
        for i, c in enumerate(chunks):
            h = hin_ref[i] * rows[0, 1:2, c]
            hst[:, c] = h
            zf[0:128, c], zf[256:384, c] = halves(h)
            g = gin_ref[i] * rows[blocks - 1, 0:1, c]
            gst[:, c] = g
            zb[0:128, c], zb[256:384, c] = halves(g)

    spanf = pl.ds(pl.multiple_of(kf * Q, Q), Q)
    spanb = pl.ds(pl.multiple_of(kb * Q, Q), Q)
    lane = iota((Q, 2 * Q), 1)
    row = iota((Q, 2 * Q), 0)

    b_f, c_f = bc_ref[spanf, :LANES], bc_ref[spanf, LANES:]
    b_b, c_b = bc_ref[spanb, :LANES], bc_ref[spanb, LANES:]
    b_ff = jnp.concatenate([b_f, b_f], axis=0)
    c_bb = jnp.concatenate([c_b, c_b], axis=0)
    zero = jnp.zeros((Q, 2 * Q), F32)

    lower = row >= lane % Q
    s_hi, s_lo = halves(jnp.where(lower, dot_nt(c_f, b_ff), zero))
    first_f = jnp.concatenate([c_f, s_hi], axis=1)
    second_f = jnp.concatenate([s_lo, c_f], axis=1)
    upper = row <= lane % Q
    s_hi, s_lo = halves(jnp.where(upper, dot_nt(b_b, c_bb), zero))
    first_b = jnp.concatenate([b_b, s_hi], axis=1)
    second_b = jnp.concatenate([s_lo, b_b], axis=1)

    for c in chunks:
        e = dot_nn(pe[spanf, :], sel[:, c])
        f = dot_nn(pf[spanf, :], sel[:, c])
        lifted = e * yf_ref[:, c].astype(F32)
        xs = f * xf_ref[:, c].astype(F32)
        zf[192:256, c], zf[128:192, c] = halves(xs)
        ll[0:64, c], ll[64:128, c] = halves(lifted)
        out = dot_nn(first_f, zf[0:256, c]) + dot_nn(second_f, zf[128:384, c])
        prods[0:64, c], prods[64:128, c] = halves(lifted * out)

        e = dot_nn(pe[spanb, :], sel[:, c])
        f = dot_nn(pf[spanb, :], sel[:, c])
        y = yb_ref[:, c].astype(F32)
        x = xb_ref[:, c].astype(F32)
        lifted = e * y
        xs = f * x
        zb[192:256, c], zb[128:192, c] = halves(lifted)
        xx[0:64, c], xx[64:128, c] = halves(xs)
        out = dot_nn(first_b, zb[0:256, c]) + dot_nn(second_b, zb[128:384, c])
        prods[128:192, c], prods[192:256, c] = halves(xs * out)
        gx_ref[:, c] = (f * out + rows[blocks, :1, c] * y).astype(BF16)
        yx[:, c] += jnp.sum((y * x).reshape(Q // 8, 8, CHUNK), axis=0)

    sums = dot_nt(prods[...], sel[...])
    vs[spanf, :] = sums[0:64] + sums[64:128]
    ws[spanb, :] = sums[128:192] + sums[192:256]

    r1 = dot_nt(ll[...], zf[0:256, :])
    r2 = dot_nt(ll[0:64, :], zf[256:384, :])
    pair = r1[:64, 128:] + r1[64:, 128:]
    pair = jnp.where(lower, pair, zero)
    p_hi, p_lo = halves(pair)
    grad_c = r1[:64, :128] + r1[64:, :128] + r2 + dot_nn(p_hi, b_ff) + dot_nn(p_lo, b_ff)
    turned = jnp.transpose(pair)
    t_hi, t_lo = halves(turned[:64] + turned[64:])
    part[spanf, LANES:] = grad_c
    part[spanf, :LANES] += dot_nn(t_hi, c_f) + dot_nn(t_lo, c_f)
    r1 = dot_nt(xx[...], zb[0:128, :])
    r2 = dot_nt(xx[0:64, :], zb[256:384, :])
    part[spanb, :LANES] += r1[:64] + r1[64:] + r2

    bt = jnp.transpose(b_ff.astype(F32)).astype(BF16)
    ct = jnp.transpose(c_bb.astype(F32)).astype(BF16)
    last = step == blocks - 1
    for c in chunks:
        come = jnp.where(last, 1.0, rows[jnp.minimum(kf + 1, blocks - 1), 1:2, c])
        h = (hst[:, c] + dot_nn(bt, zf[128:256, c])) * rows[kf, 0:1, c] * come
        hst[:, c] = h
        zf[0:128, c], zf[256:384, c] = halves(h)
        g = (gst[:, c] + dot_nn(ct, zb[128:256, c])) * rows[kb, 1:2, c] * rows[jnp.maximum(kb - 1, 0), 0:1, c]
        gst[:, c] = g
        zb[0:128, c], zb[256:384, c] = halves(g)

    @pl.when(step == half)
    def _():
        pl.semaphore_wait(barrier, zs - 1 + flats - 1)

    @pl.when(step >= half)
    def _():
        j = step - half
        for q in range(zs):
            stage[j, q, :lines] = part[pl.ds(pl.multiple_of(kf * Q + q * lines, lines), lines), :]
            stage[j, q, lines:] = part[pl.ds(pl.multiple_of(kb * Q + q * lines, lines), lines), :]
        for d in range(1, zs):
            scatter(j, d).start()

    @pl.when(step >= half + 1)
    def _():
        reduce_pair(step - half - 1)

    @pl.when(step >= half + 2)
    def _():
        finish_pair(step - half - 2)

    @pl.when(step == blocks - 1)
    def _():
        closing = jnp.concatenate(
            [jnp.sum(gin_ref[i] * hst[:, c], axis=0, keepdims=True) for i, c in enumerate(chunks)], axis=1)
        totals = jnp.concatenate([closing, jnp.sum(yx[...], axis=0, keepdims=True), jnp.zeros((14, width), F32)], axis=0)
        hi, lo = halves(totals)
        totals = dot_nt(hi, sel[...]) + dot_nt(lo, sel[...])
        after = totals[0:1]
        gdts = []
        tri = triangle(True)
        d_alog = jnp.zeros((1, LANES), F32)
        d_bias = jnp.zeros((1, LANES), F32)
        for k in reversed(range(blocks)):
            span = slice(k * Q, (k + 1) * Q)
            w = ws[span]
            dt = dts[span]
            dlog = dot_nn(tri, vs[span] - w, HIGH) + after
            after = dlog[0:1]
            grad_dt = (w / dt + dlog * rate) * jax.nn.sigmoid(shs[span])
            gdts.append(grad_dt)
            d_alog = d_alog + jnp.sum(dlog * dt, axis=0, keepdims=True)
            d_bias = d_bias + jnp.sum(grad_dt, axis=0, keepdims=True)
        hsum[...] = jnp.concatenate([d_alog * rate, d_bias, totals[1:2], jnp.zeros((5, LANES), F32)], axis=0)

        @pl.loop(1, flats)
        def _(d):
            share(d).start()

        reduce_pair(half - 1)
        gdt_ref[...] = jnp.transpose(jnp.concatenate(gdts[::-1], axis=0))[:heads]
        finish_pair(half - 2)
        hgot[flat] = hsum[...]

        @pl.loop(1, flats)
        def _(d):
            share_in(d).wait_recv()

        total = hgot[0]
        for other in range(1, flats):
            total = total + hgot[other]
        gheads_ref[...] = total * scale
        finish_pair(half - 1)

        @pl.loop(1, flats)
        def _(d):
            share(d).wait_send()

        @pl.loop(0, half)
        def _(j):
            for d in range(1, zs):
                scatter(j, d).wait_send()
                gather(j, d).wait_send()


def main(x, y, bc, dt, bias, alog, skip, hin, gin):
    length, width = x.shape
    heads = dt.shape[0]
    state = bc.shape[1] // 2
    blocks = length // Q
    zs, dps = lax.axis_size("head"), lax.axis_size("dp")
    flats = lax.axis_size("seq") * dps
    scale = 1.0 / math.sqrt(flats * length)
    lines = Q // zs
    dma = pltpu.SemaphoreType.DMA
    whole = pl.BlockSpec(memory_space=pltpu.VMEM)
    ahead = pl.BlockSpec((Q, width), lambda i: (i, 0))
    back = pl.BlockSpec((Q, width), lambda i: (blocks - 1 - i, 0))
    return pl.pallas_call(
        functools.partial(main_kernel, heads, zs, dps, flats, scale),
        grid=(blocks,),
        out_shape=(
            jax.ShapeDtypeStruct((length, width), BF16),
            jax.ShapeDtypeStruct((length, 2 * state), F32),
            jax.ShapeDtypeStruct((heads, length), F32),
            jax.ShapeDtypeStruct((8, LANES), F32),
        ),
        in_specs=[ahead, ahead, back, back] + [whole] * 7,
        out_specs=(back, whole, whole, whole),
        scratch_shapes=[
            pltpu.VMEM((length, LANES), BF16),
            pltpu.VMEM((length, LANES), BF16),
            pltpu.VMEM((length, LANES), F32),
            pltpu.VMEM((length, LANES), F32),
            pltpu.VMEM((LANES, width), BF16),
            pltpu.VMEM((blocks + 1, 8, width), F32),
            pltpu.VMEM((length, LANES), F32),
            pltpu.VMEM((length, LANES), F32),
            pltpu.VMEM((384, width), BF16),
            pltpu.VMEM((384, width), BF16),
            pltpu.VMEM((128, width), BF16),
            pltpu.VMEM((128, width), BF16),
            pltpu.VMEM((256, width), BF16),
            pltpu.VMEM((state, width), F32),
            pltpu.VMEM((state, width), F32),
            pltpu.VMEM((8, width), F32),
            pltpu.VMEM((length, 2 * state), F32),
            pltpu.VMEM((blocks // 2, zs, 2 * lines, 2 * state), F32),
            pltpu.VMEM((blocks // 2, zs, 2 * lines, 2 * state), F32),
            pltpu.VMEM((blocks // 2, zs, 2 * lines, 2 * state), F32),
            pltpu.VMEM((8, LANES), F32),
            pltpu.VMEM((flats, 8, LANES), F32),
            dma((blocks // 2, zs)), dma((blocks // 2, zs)),
            dma((blocks // 2, zs)), dma((blocks // 2, zs)),
            dma((flats,)), dma((flats,)),
        ],
        compiler_params=pltpu.CompilerParams(
            vmem_limit_bytes=VMEM_LIMIT, collective_id=1, has_side_effects=True, dimension_semantics=("arbitrary",)),
        cost_estimate=pl.CostEstimate(flops=60 * length * width * state, bytes_accessed=12 * length * width, transcendentals=0),
    )(x, y, x, y, bc, dt, bias, alog, skip, hin, gin)


def shards(inputs_x, inputs_bc, dt_raw, grad_out, a_log, dt_bias, skip):
    heads = a_log.shape[0]
    x, y, bc, dt = inputs_x[0], grad_out[0], inputs_bc[0], dt_raw[0].T
    bias, alog, skips = dt_bias[None], a_log[None], skip[None]
    hin, gin = edges(x, y, bc, dt, bias, alog)
    grad_x, grad_bc, grad_dt, sums = main(x, y, bc, dt, bias, alog, skips, hin, gin)
    return (grad_x[None], grad_bc[None], grad_dt.T[None], sums[:3, :heads])


def solution(mesh):
    placed = (
        P("dp", "seq", "head"),
        P("dp", "seq", None),
        P("dp", "seq", "head"),
        P("dp", "seq", "head"),
        P("head"),
        P("head"),
        P("head"),
    )
    return jax.shard_map(
        shards,
        mesh=mesh,
        in_specs=placed,
        out_specs=(
            P("dp", "seq", "head"),
            P("dp", "seq", None),
            P("dp", "seq", "head"),
            P(None, "head"),
        ),
        check_vma=False,
    )
```

```python
import functools
import math

import jax
import jax.numpy as jnp
from jax import lax
from jax.experimental import pallas as pl
from jax.experimental.pallas import tpu as pltpu
from jax.sharding import PartitionSpec as P

Q = 64
CHUNK = 256
HEADDIM = 64
LANES = 128
HIGH = lax.Precision.HIGHEST
F32 = jnp.float32
BF16 = jnp.bfloat16
VMEM_LIMIT = 56 * 1024 * 1024


def dot_nn(a, b, precision=None):
    return lax.dot_general(a, b, (((1,), (0,)), ((), ())), precision=precision, preferred_element_type=F32)


def dot_nt(a, b):
    return lax.dot_general(a, b, (((1,), (1,)), ((), ())), preferred_element_type=F32)


def halves(value):
    hi = value.astype(BF16)
    return hi, (value - hi.astype(F32)).astype(BF16)


def iota(shape, dim):
    return lax.broadcasted_iota(jnp.int32, shape, dim)


def triangle(upper):
    r, c = iota((Q, Q), 0), iota((Q, Q), 1)
    return jnp.where(r <= c if upper else r >= c, 1.0, 0.0).astype(F32)


def repeat_heads(value, heads):
    pick = jnp.where(iota((heads, LANES), 1) % heads == iota((heads, LANES), 0), 1.0, 0.0)
    return dot_nn(value, pick.astype(F32), HIGH)


def packed(value, heads, terms):
    lane = iota(value.shape, 1)
    total = jnp.zeros_like(value)
    rest = value
    for term in range(terms):
        part = rest.astype(BF16).astype(F32)
        total = jnp.where((lane >= term * heads) & (lane < (term + 1) * heads), part, total)
        rest = rest - part
    return total.astype(BF16)


def head_lanes(heads, width):
    shape = (LANES, width)
    return jnp.where(iota(shape, 0) % heads == iota(shape, 1) // HEADDIM, 1.0, 0.0).astype(BF16)


def steps_of(dt_ref, bias_ref, heads):
    turned = jnp.transpose(jnp.concatenate([dt_ref[...]] * (LANES // heads), axis=0))
    return turned + repeat_heads(jnp.broadcast_to(bias_ref[...], (8, heads)), heads)[:1]


def rates_of(alog_ref, heads):
    return -jnp.exp(repeat_heads(jnp.broadcast_to(alog_ref[...], (8, heads)), heads))[:1]


def edges_kernel(heads, x_ref, y_ref, bc_ref, dt_ref, bias_ref, alog_ref,
                 hin_ref, gin_ref, skip_ref, xo_ref, lo_ref, fo_ref, af_ref, ab_ref, part_ref,
                 pe, pf, le, lf, bt, ct, sel, xb, yb, xs, ys, dec, mine, out0, got0, chip, gath, pre, inc, fin,
                 xbuf, lbuf, fbuf, abuf, bbuf, part, yx,
                 load_sem, s0, r0, s1, r1, s2, r2, s3, r3, put_sem, put_one):
    length = bc_ref.shape[0]
    blocks = length // Q
    groups = hin_ref.shape[0]
    state = hin_ref.shape[1]
    me = lax.axis_index("seq")
    core = lax.rem(me, 2)
    place = me // 2
    ahead = core == 1
    partner = me + 1 - 2 * core

    def peer(d):
        return lax.rem(place + d, groups)

    def loads(i):
        g = peer(1 + i)
        span = pl.ds(pl.multiple_of(g * CHUNK, CHUNK), CHUNK)
        return (pltpu.make_async_copy(x_ref.at[:, span], xb.at[i], load_sem.at[0, i]),
                pltpu.make_async_copy(y_ref.at[:, span], yb.at[i], load_sem.at[1, i]))

    def swap(i):
        return pltpu.make_async_remote_copy(
            src_ref=out0.at[i], dst_ref=got0.at[i], send_sem=s0.at[i], recv_sem=r0.at[i],
            device_id={"seq": partner}, device_id_type=pl.DeviceIdType.MESH)

    def spread(d):
        return pltpu.make_async_remote_copy(
            src_ref=chip.at[d - 1], dst_ref=gath.at[place], send_sem=s1.at[d - 1], recv_sem=r1.at[place],
            device_id={"seq": peer(d) * 2 + core}, device_id_type=pl.DeviceIdType.MESH)

    def spread_in(source):
        return pltpu.make_async_remote_copy(
            src_ref=chip.at[0], dst_ref=gath.at[source], send_sem=s1.at[0], recv_sem=r1.at[source],
            device_id={"seq": source * 2 + core}, device_id_type=pl.DeviceIdType.MESH)

    def back(pos):
        return pltpu.make_async_remote_copy(
            src_ref=pre.at[pos], dst_ref=inc.at[place], send_sem=s2.at[pos], recv_sem=r2.at[place],
            device_id={"seq": pos * 2 + core}, device_id_type=pl.DeviceIdType.MESH)

    def back_in(source):
        return pltpu.make_async_remote_copy(
            src_ref=pre.at[source], dst_ref=inc.at[source], send_sem=s2.at[source], recv_sem=r2.at[source],
            device_id={"seq": source * 2 + core}, device_id_type=pl.DeviceIdType.MESH)

    def hand(g):
        return pltpu.make_async_remote_copy(
            src_ref=inc.at[g], dst_ref=fin.at[g], send_sem=s3.at[g], recv_sem=r3.at[g],
            device_id={"seq": partner}, device_id_type=pl.DeviceIdType.MESH)

    for i in range(groups):
        for copy in loads(i):
            copy.start()
    barrier = pltpu.get_barrier_semaphore()
    pl.semaphore_signal(barrier, inc=1, device_id={"seq": partner}, device_id_type=pl.DeviceIdType.MESH)
    for d in range(1, groups):
        pl.semaphore_signal(barrier, inc=1, device_id={"seq": peer(d) * 2 + core}, device_id_type=pl.DeviceIdType.MESH)

    sel[...] = head_lanes(heads, sel.shape[1])
    rate = rates_of(alog_ref, heads)
    dt = jax.nn.softplus(steps_of(dt_ref, bias_ref, heads))
    tri = triangle(False)
    cums = [dot_nn(tri, dt[k * Q:(k + 1) * Q] * rate, HIGH) for k in range(blocks)]
    before = jnp.zeros((1, LANES), F32)
    for k in range(blocks):
        mid = cums[k][Q // 2 - 1:Q // 2]
        le[pl.ds(k * Q, Q), :] = packed(jnp.exp(cums[k] - mid), heads, 2)
        lf[pl.ds(k * Q, Q), :] = packed(dt[k * Q:(k + 1) * Q] * jnp.exp(mid - cums[k]), heads, 2)
        pe[pl.ds(k * Q, Q), :] = packed(jnp.exp(cums[k] + before), heads, 2)
        before = before + cums[k][Q - 1:Q]
    after = jnp.zeros((1, LANES), F32)
    for k in reversed(range(blocks)):
        last = cums[k][Q - 1:Q]
        pf[pl.ds(k * Q, Q), :] = packed(dt[k * Q:(k + 1) * Q] * jnp.exp((last - cums[k]) + after), heads, 2)
        after = after + last
    dec[...] = packed(jnp.broadcast_to(jnp.exp(before), (8, LANES)), heads, 3)
    b_t = jnp.transpose(bc_ref[:, :LANES].astype(F32)).astype(BF16)
    c_t = jnp.transpose(bc_ref[:, LANES:].astype(F32)).astype(BF16)
    bt[:, :length] = b_t
    bt[:, length:] = b_t
    ct[:, :length] = c_t
    ct[:, length:] = c_t
    pl.semaphore_wait(barrier, groups)

    def combine(i):
        swap(i).wait_recv()
        keep = out0[i, state:state + 1, :]
        value = mine[i] + keep * got0[i, :state, :]
        decay = out0[i, state:, :] * got0[i, state:, :]
        if i < groups - 1:
            chip[i, :state, :] = value
            chip[i, state:, :] = decay
            spread(i + 1).start()
        else:
            gath[place, :state, :] = value
            gath[place, state:, :] = decay

    for i in range(groups):
        g = peer(1 + i)
        here = sel[:, pl.ds(pl.multiple_of(g * CHUNK, CHUNK), CHUNK)]
        copy_x, copy_y = loads(i)
        copy_x.wait()
        hi, lo = halves(dot_nn(pf[...], here) * xb[i].astype(F32))
        xs[:length] = hi
        xs[length:] = lo
        ends = dot_nn(bt[...], xs[...])
        copy_y.wait()
        hi, lo = halves(dot_nn(pe[...], here) * yb[i].astype(F32))
        ys[:length] = hi
        ys[length:] = lo
        starts = dot_nn(ct[...], ys[...])
        mine[i] = jnp.where(ahead, ends, starts)
        out0[i, :state, :] = jnp.where(ahead, starts, ends)
        out0[i, state:, :] = dot_nn(dec[...], here)
        swap(i).start()
        if i:
            combine(i - 1)
    combine(groups - 1)

    def scan():
        total = jnp.zeros((state, CHUNK), F32)
        for d in range(1, groups):
            spread_in(peer(d)).wait_recv()
        for k in range(groups):
            pos = jnp.where(ahead, k, groups - 1 - k)

            @pl.when(pos == place)
            def _():
                inc[place] = total

            @pl.when(pos != place)
            def _():
                pre[pos] = total
                back(pos).start()

            total = gath[pos, state:state + 1, :] * total + gath[pos, :state, :]

    def puts(i):
        g = peer(1 + i)
        span = pl.ds(pl.multiple_of(g * CHUNK, CHUNK), CHUNK)
        return (pltpu.make_async_copy(xbuf.at[:, :, span], xo_ref.at[:, :, span], put_sem.at[0, i]),
                pltpu.make_async_copy(lbuf.at[:, :, span], lo_ref.at[:, :, span], put_sem.at[1, i]),
                pltpu.make_async_copy(fbuf.at[:, span], fo_ref.at[:, span], put_sem.at[2, i]))

    for i in range(groups):
        g = peer(1 + i)
        span = pl.ds(pl.multiple_of(g * CHUNK, CHUNK), CHUNK)
        here = sel[:, span]
        x = xb[i].astype(F32)
        y = yb[i].astype(F32)
        f = dot_nn(lf[...], here)
        fbuf[:, span] = f
        hi, lo = halves(f * x)
        xbuf[:, :Q, span] = lo.reshape(blocks, Q, CHUNK)
        xbuf[:, Q:, span] = hi.reshape(blocks, Q, CHUNK)
        hi, lo = halves(dot_nn(le[...], here) * y)
        lbuf[:, :Q, span] = lo.reshape(blocks, Q, CHUNK)
        lbuf[:, Q:, span] = hi.reshape(blocks, Q, CHUNK)
        yx[:, span] = jnp.sum((y * x).reshape(length // 8, 8, CHUNK), axis=0)
        for copy in puts(i):
            copy.start()
        if i == groups // 2:
            scan()

    lane = iota((Q, 2 * Q), 1)
    row = iota((Q, 2 * Q), 0)
    none = jnp.zeros((Q, 2 * Q), F32)

    @pl.loop(0, blocks)
    def _(k):
        span = pl.ds(pl.multiple_of(k * Q, Q), Q)
        b, c = bc_ref[span, :LANES], bc_ref[span, LANES:]
        bb = jnp.concatenate([b, b], axis=0)
        cc = jnp.concatenate([c, c], axis=0)
        lower = row >= lane % Q
        for dest, one, two, keep in ((abuf, c, bb, lower), (bbuf, b, cc, row <= lane % Q)):
            s_hi, s_lo = halves(jnp.where(keep, dot_nt(one, two), none))
            dest[k, :Q, :2 * Q] = one
            dest[k, :Q, 2 * Q:] = s_hi
            dest[k, Q:3 * Q, :2 * Q] = jnp.zeros((2 * Q, 2 * Q), BF16)
            dest[k, Q:3 * Q, 2 * Q:] = jnp.transpose(two.astype(F32)).astype(BF16)
            dest[k, 3 * Q:, :2 * Q] = s_lo
            dest[k, 3 * Q:, 2 * Q:] = one
        r = dot_nt(lbuf[k], xbuf[k])
        pair = jnp.where(lower, r[:Q] + r[Q:], none)
        p_hi, p_lo = halves(pair)
        part[span, LANES:] = dot_nn(p_hi, bb) + dot_nn(p_lo, bb)
        turned = jnp.transpose(pair)
        t_hi, t_lo = halves(turned[:Q] + turned[Q:])
        part[span, :LANES] = dot_nn(t_hi, c) + dot_nn(t_lo, c)

    put_all = (pltpu.make_async_copy(abuf, af_ref, put_one.at[0]),
               pltpu.make_async_copy(bbuf, ab_ref, put_one.at[1]),
               pltpu.make_async_copy(part, part_ref, put_one.at[2]))
    for copy in put_all:
        copy.start()
    sums = jnp.sum(yx[...], axis=0, keepdims=True)
    hi, lo = halves(jnp.broadcast_to(sums, yx.shape))
    skip_ref[...] = dot_nt(hi, sel[...]) + dot_nt(lo, sel[...])

    for d in range(groups):
        g = peer(d)
        if d:
            back_in(g).wait_recv()
        hand(g).start()
    for d in range(groups):
        g = peer(d)
        i = (d - 1) % groups
        own = got0[i, state:state + 1, :] * inc[g] + got0[i, :state, :]
        hand(g).wait_recv()
        other = fin[g]
        hin_ref[g] = jnp.where(ahead, own, other)
        gin_ref[g] = jnp.where(ahead, other, own)
    for i in range(groups):
        swap(i).wait_send()
        hand(i).wait_send()
    for d in range(1, groups):
        spread(d).wait_send()
        back(peer(d)).wait_send()
    for i in range(groups):
        for copy in puts(i):
            copy.wait()
    for copy in put_all:
        copy.wait()


def edges(x, y, bc, dt, bias, alog):
    length, width = x.shape
    heads = dt.shape[0]
    state = bc.shape[1] // 2
    groups = width // CHUNK
    blocks = length // Q
    whole = pl.BlockSpec(memory_space=pltpu.VMEM)
    anywhere = pl.BlockSpec(memory_space=pl.ANY)
    dma = pltpu.SemaphoreType.DMA
    return pl.pallas_call(
        functools.partial(edges_kernel, heads),
        out_shape=(
            jax.ShapeDtypeStruct((groups, state, CHUNK), F32),
            jax.ShapeDtypeStruct((groups, state, CHUNK), F32),
            jax.ShapeDtypeStruct((8, LANES), F32),
            jax.ShapeDtypeStruct((blocks, 2 * Q, width), BF16),
            jax.ShapeDtypeStruct((blocks, 2 * Q, width), BF16),
            jax.ShapeDtypeStruct((length, width), F32),
            jax.ShapeDtypeStruct((blocks, 4 * Q, 4 * Q), BF16),
            jax.ShapeDtypeStruct((blocks, 4 * Q, 4 * Q), BF16),
            jax.ShapeDtypeStruct((length, 2 * state), F32),
        ),
        in_specs=[anywhere, anywhere, whole, whole, whole, whole],
        out_specs=(whole, whole, whole) + (anywhere,) * 6,
        scratch_shapes=[
            pltpu.VMEM((length, LANES), BF16),
            pltpu.VMEM((length, LANES), BF16),
            pltpu.VMEM((length, LANES), BF16),
            pltpu.VMEM((length, LANES), BF16),
            pltpu.VMEM((state, 2 * length), BF16),
            pltpu.VMEM((state, 2 * length), BF16),
            pltpu.VMEM((LANES, width), BF16),
            pltpu.VMEM((groups, length, CHUNK), BF16),
            pltpu.VMEM((groups, length, CHUNK), BF16),
            pltpu.VMEM((2 * length, CHUNK), BF16),
            pltpu.VMEM((2 * length, CHUNK), BF16),
            pltpu.VMEM((8, LANES), BF16),
            pltpu.VMEM((groups, state, CHUNK), F32),
            pltpu.VMEM((groups, state + 8, CHUNK), F32),
            pltpu.VMEM((groups, state + 8, CHUNK), F32),
            pltpu.VMEM((groups - 1, state + 8, CHUNK), F32),
            pltpu.VMEM((groups, state + 8, CHUNK), F32),
            pltpu.VMEM((groups, state, CHUNK), F32),
            pltpu.VMEM((groups, state, CHUNK), F32),
            pltpu.VMEM((groups, state, CHUNK), F32),
            pltpu.VMEM((blocks, 2 * Q, width), BF16),
            pltpu.VMEM((blocks, 2 * Q, width), BF16),
            pltpu.VMEM((length, width), F32),
            pltpu.VMEM((blocks, 4 * Q, 4 * Q), BF16),
            pltpu.VMEM((blocks, 4 * Q, 4 * Q), BF16),
            pltpu.VMEM((length, 2 * state), F32),
            pltpu.VMEM((8, width), F32),
            dma((2, groups)),
            dma((groups,)), dma((groups,)),
            dma((groups,)), dma((groups,)),
            dma((groups,)), dma((groups,)),
            dma((groups,)), dma((groups,)),
            dma((3, groups)), dma((3,)),
        ],
        compiler_params=pltpu.CompilerParams(vmem_limit_bytes=VMEM_LIMIT, collective_id=0, has_side_effects=True),
        cost_estimate=pl.CostEstimate(flops=8 * length * width * state, bytes_accessed=4 * length * width, transcendentals=0),
    )(x, y, bc, dt, bias, alog)


def main_kernel(heads, zs, dps, flats, scale, xf_ref, lf_ref, xb_ref, lb_ref, fb_ref, yb_ref, af_ref, ab_ref,
                part_ref, dskip_ref, dt_ref, bias_ref, alog_ref, skip_ref, hin_ref, gin_ref,
                gx_ref, gbc_ref, gdt_ref, gheads_ref,
                dts, shs, sel, rows, vs, ws, hz, gz, prods, hst, gst,
                stage, landed, done, hsum, hgot, s1, r1s, s2, r2s, s3, r3s):
    length = dts.shape[0]
    width = sel.shape[1]
    blocks = length // Q
    step = pl.program_id(0)
    kf = step
    kb = blocks - 1 - step
    chunks = [slice(c * CHUNK, (c + 1) * CHUNK) for c in range(width // CHUNK)]
    rate = rates_of(alog_ref, heads)
    lines = Q // zs
    z = lax.axis_index("head")
    flat = lax.axis_index("seq") * dps + lax.axis_index("dp")
    barrier = pltpu.get_barrier_semaphore()

    def zpeer(d):
        return {"head": lax.rem(z + d, zs)}

    def fpeer(d):
        other = lax.rem(flat + d, flats)
        return {"seq": other // dps, "dp": lax.rem(other, dps)}

    def scatter(j, d):
        q = lax.rem(z + d, zs)
        return pltpu.make_async_remote_copy(
            src_ref=stage.at[j, q], dst_ref=landed.at[j, z], send_sem=s1.at[j, q], recv_sem=r1s.at[j, z],
            device_id=zpeer(d), device_id_type=pl.DeviceIdType.MESH)

    def scatter_in(j, d):
        q = lax.rem(z + d, zs)
        return pltpu.make_async_remote_copy(
            src_ref=stage.at[j, q], dst_ref=landed.at[j, q], send_sem=s1.at[j, q], recv_sem=r1s.at[j, q],
            device_id=zpeer(d), device_id_type=pl.DeviceIdType.MESH)

    def gather(j, d):
        q = lax.rem(z + d, zs)
        return pltpu.make_async_remote_copy(
            src_ref=done.at[j, z], dst_ref=done.at[j, z], send_sem=s2.at[j, q], recv_sem=r2s.at[j, z],
            device_id=zpeer(d), device_id_type=pl.DeviceIdType.MESH)

    def gather_in(j, d):
        q = lax.rem(z + d, zs)
        return pltpu.make_async_remote_copy(
            src_ref=done.at[j, q], dst_ref=done.at[j, q], send_sem=s2.at[j, q], recv_sem=r2s.at[j, q],
            device_id=zpeer(d), device_id_type=pl.DeviceIdType.MESH)

    def share(d):
        return pltpu.make_async_remote_copy(
            src_ref=hsum, dst_ref=hgot.at[flat], send_sem=s3.at[d], recv_sem=r3s.at[flat],
            device_id=fpeer(d), device_id_type=pl.DeviceIdType.MESH)

    def share_in(d):
        other = lax.rem(flat + d, flats)
        return pltpu.make_async_remote_copy(
            src_ref=hsum, dst_ref=hgot.at[other], send_sem=s3.at[d], recv_sem=r3s.at[other],
            device_id=fpeer(d), device_id_type=pl.DeviceIdType.MESH)

    def reduce_pair(j):
        for d in range(1, zs):
            scatter_in(j, d).wait_recv()
        landed[j, z] = stage[j, z]
        total = landed[j, 0]
        for q in range(1, zs):
            total = total + landed[j, q]
        done[j, z] = total
        for d in range(1, zs):
            gather(j, d).start()

    def finish_pair(j):
        for d in range(1, zs):
            gather_in(j, d).wait_recv()
        for q in range(zs):
            gbc_ref[pl.ds(pl.multiple_of(j * Q + q * lines, lines), lines), LANES:] = done[j, q, :lines]
            gbc_ref[pl.ds(pl.multiple_of((blocks - 1 - j) * Q + q * lines, lines), lines), :LANES] = done[j, q, lines:]

    @pl.when(step == 0)
    def _():
        for d in range(1, zs):
            pl.semaphore_signal(barrier, inc=1, device_id=zpeer(d), device_id_type=pl.DeviceIdType.MESH)

        @pl.loop(1, flats)
        def _(d):
            pl.semaphore_signal(barrier, inc=1, device_id=fpeer(d), device_id_type=pl.DeviceIdType.MESH)

        sel[...] = head_lanes(heads, width)
        shifted = steps_of(dt_ref, bias_ref, heads)
        shs[...] = shifted
        dt = jax.nn.softplus(shifted)
        dts[...] = dt
        tri = triangle(False)
        mids, lasts = [], []
        for k in range(blocks):
            here = dt[k * Q:(k + 1) * Q]
            cum = dot_nn(tri, here * rate, HIGH)
            mid = cum[Q // 2 - 1:Q // 2]
            mids.append(mid)
            lasts.append(cum[Q - 1:Q])
        for k in range(blocks):
            gone = jnp.broadcast_to(jnp.exp(lasts[k] - mids[k]), (8, LANES))
            come = jnp.broadcast_to(jnp.exp(mids[k]), (8, LANES))
            factor = packed(jnp.where(iota((8, LANES), 0) == 0, gone, come), heads, 3)
            rows[k] = dot_nn(factor, sel[...])
        skips = repeat_heads(jnp.broadcast_to(skip_ref[...], (8, heads)), heads)
        rows[blocks] = dot_nn(packed(skips, heads, 3), sel[...])
        for i, c in enumerate(chunks):
            h = hin_ref[i] * rows[0, 1:2, c]
            hst[:, c] = h
            hz[0, :128, c], hz[0, 128:, c] = halves(h)
            g = gin_ref[i] * rows[blocks - 1, 0:1, c]
            gst[:, c] = g
            gz[0, :128, c], gz[0, 128:, c] = halves(g)

    spanf = pl.ds(pl.multiple_of(kf * Q, Q), Q)
    spanb = pl.ds(pl.multiple_of(kb * Q, Q), Q)
    now = lax.rem(step, 2)
    first_f, second_f = af_ref[0, :192], af_ref[0, 192:]
    first_b, second_b = ab_ref[0, :192], ab_ref[0, 192:]
    come_f = jnp.minimum(kf + 1, blocks - 1)
    come_b = jnp.maximum(kb - 1, 0)
    last = step == blocks - 1
    for c in chunks:
        wide = xf_ref[0, :, c]
        one = dot_nn(first_f, jnp.concatenate([hz[now, :128, c], wide], axis=0))
        two = dot_nn(second_f, jnp.concatenate([wide, hz[now, 128:, c]], axis=0))
        lifted = lf_ref[0, 64:, c].astype(F32) + lf_ref[0, :64, c].astype(F32)
        prods[0:64, c], prods[64:128, c] = halves(lifted * (one[:64] + two))
        h = (hst[:, c] + one[64:]) * rows[kf, 0:1, c] * jnp.where(last, 1.0, rows[come_f, 1:2, c])
        hst[:, c] = h
        hz[1 - now, :128, c], hz[1 - now, 128:, c] = halves(h)

        wide = lb_ref[0, :, c]
        one = dot_nn(first_b, jnp.concatenate([gz[now, :128, c], wide], axis=0))
        two = dot_nn(second_b, jnp.concatenate([wide, gz[now, 128:, c]], axis=0))
        out = one[:64] + two
        xs = xb_ref[0, 64:, c].astype(F32) + xb_ref[0, :64, c].astype(F32)
        prods[128:192, c], prods[192:256, c] = halves(xs * out)
        gx_ref[:, c] = (fb_ref[:, c] * out + rows[blocks, :1, c] * yb_ref[:, c].astype(F32)).astype(BF16)
        g = (gst[:, c] + one[64:]) * rows[kb, 1:2, c] * rows[come_b, 0:1, c]
        gst[:, c] = g
        gz[1 - now, :128, c], gz[1 - now, 128:, c] = halves(g)

    sums = dot_nt(prods[...], sel[...])
    vs[spanf, :] = sums[0:64] + sums[64:128]
    ws[spanb, :] = sums[128:192] + sums[192:256]
    r = dot_nt(hz[now], lf_ref[0])
    turned = jnp.transpose(r[:128] + r[128:])
    grad_c = part_ref[spanf, LANES:] + turned[:64] + turned[64:]
    r = dot_nt(gz[now], xb_ref[0])
    turned = jnp.transpose(r[:128] + r[128:])
    grad_b = part_ref[spanb, :LANES] + turned[:64] + turned[64:]
    stage[step, :, :lines] = grad_c.reshape(zs, lines, LANES)
    stage[step, :, lines:] = grad_b.reshape(zs, lines, LANES)

    @pl.when(step == 0)
    def _():
        pl.semaphore_wait(barrier, zs - 1 + flats - 1)

    for d in range(1, zs):
        scatter(step, d).start()

    @pl.when(step >= 1)
    def _():
        reduce_pair(step - 1)

    @pl.when(step >= 2)
    def _():
        finish_pair(step - 2)

    @pl.when(step == blocks - 1)
    def _():
        closing = jnp.concatenate(
            [jnp.sum(gin_ref[i] * hst[:, c], axis=0, keepdims=True) for i, c in enumerate(chunks)], axis=1)
        hi, lo = halves(jnp.broadcast_to(closing, (16, width)))
        totals = dot_nt(hi, sel[...]) + dot_nt(lo, sel[...])
        after = totals[0:1]
        gdts = []
        tri = triangle(True)
        d_alog = jnp.zeros((1, LANES), F32)
        d_bias = jnp.zeros((1, LANES), F32)
        for k in reversed(range(blocks)):
            span = slice(k * Q, (k + 1) * Q)
            w = ws[span]
            dt = dts[span]
            dlog = dot_nn(tri, vs[span] - w, HIGH) + after
            after = dlog[0:1]
            grad_dt = (w / dt + dlog * rate) * jax.nn.sigmoid(shs[span])
            gdts.append(grad_dt)
            d_alog = d_alog + jnp.sum(dlog * dt, axis=0, keepdims=True)
            d_bias = d_bias + jnp.sum(grad_dt, axis=0, keepdims=True)
        hsum[...] = jnp.concatenate([d_alog * rate, d_bias, dskip_ref[0:1], jnp.zeros((5, LANES), F32)], axis=0)

        @pl.loop(1, flats)
        def _(d):
            share(d).start()

        reduce_pair(blocks - 1)
        gdt_ref[...] = jnp.transpose(jnp.concatenate(gdts[::-1], axis=0))[:heads]
        finish_pair(blocks - 2)
        hgot[flat] = hsum[...]

        @pl.loop(1, flats)
        def _(d):
            share_in(d).wait_recv()

        total = hgot[0]
        for other in range(1, flats):
            total = total + hgot[other]
        gheads_ref[...] = total[:3, :heads] * scale
        finish_pair(blocks - 1)

        @pl.loop(1, flats)
        def _(d):
            share(d).wait_send()

        @pl.loop(0, blocks)
        def _(j):
            for d in range(1, zs):
                scatter(j, d).wait_send()
                gather(j, d).wait_send()


def main(y, dt, bias, alog, skip, hin, gin, dskip, xs, ls, fs, af, ab, part):
    length, width = y.shape
    heads = dt.shape[0]
    state = hin.shape[1]
    blocks = length // Q
    zs, dps = lax.axis_size("head"), lax.axis_size("dp")
    flats = lax.axis_size("seq") * dps
    scale = 1.0 / math.sqrt(flats * length)
    lines = Q // zs
    dma = pltpu.SemaphoreType.DMA
    whole = pl.BlockSpec(memory_space=pltpu.VMEM)
    back = pl.BlockSpec((Q, width), lambda i: (blocks - 1 - i, 0))
    pair_f = pl.BlockSpec((1, 2 * Q, width), lambda i: (i, 0, 0))
    pair_b = pl.BlockSpec((1, 2 * Q, width), lambda i: (blocks - 1 - i, 0, 0))
    left_f = pl.BlockSpec((1, 4 * Q, 4 * Q), lambda i: (i, 0, 0))
    left_b = pl.BlockSpec((1, 4 * Q, 4 * Q), lambda i: (blocks - 1 - i, 0, 0))
    return pl.pallas_call(
        functools.partial(main_kernel, heads, zs, dps, flats, scale),
        grid=(blocks,),
        out_shape=(
            jax.ShapeDtypeStruct((length, width), BF16),
            jax.ShapeDtypeStruct((length, 2 * state), F32),
            jax.ShapeDtypeStruct((heads, length), F32),
            jax.ShapeDtypeStruct((3, heads), F32),
        ),
        in_specs=[pair_f, pair_f, pair_b, pair_b, back, back, left_f, left_b] + [whole] * 8,
        out_specs=(back, whole, whole, whole),
        scratch_shapes=[
            pltpu.VMEM((length, LANES), F32),
            pltpu.VMEM((length, LANES), F32),
            pltpu.VMEM((LANES, width), BF16),
            pltpu.VMEM((blocks + 1, 8, width), F32),
            pltpu.VMEM((length, LANES), F32),
            pltpu.VMEM((length, LANES), F32),
            pltpu.VMEM((2, 256, width), BF16),
            pltpu.VMEM((2, 256, width), BF16),
            pltpu.VMEM((256, width), BF16),
            pltpu.VMEM((state, width), F32),
            pltpu.VMEM((state, width), F32),
            pltpu.VMEM((blocks, zs, 2 * lines, state), F32),
            pltpu.VMEM((blocks, zs, 2 * lines, state), F32),
            pltpu.VMEM((blocks, zs, 2 * lines, state), F32),
            pltpu.VMEM((8, LANES), F32),
            pltpu.VMEM((flats, 8, LANES), F32),
            dma((blocks, zs)), dma((blocks, zs)),
            dma((blocks, zs)), dma((blocks, zs)),
            dma((flats,)), dma((flats,)),
        ],
        compiler_params=pltpu.CompilerParams(
            vmem_limit_bytes=VMEM_LIMIT, collective_id=1, has_side_effects=True, dimension_semantics=("arbitrary",)),
        cost_estimate=pl.CostEstimate(flops=60 * length * width * state, bytes_accessed=12 * length * width, transcendentals=0),
    )(xs, ls, xs, ls, fs, y, af, ab, part, dskip, dt, bias, alog, skip, hin, gin)


def shards(inputs_x, inputs_bc, dt_raw, grad_out, a_log, dt_bias, skip):
    heads = a_log.shape[0]
    x, y, bc, dt = inputs_x[0], grad_out[0], inputs_bc[0], dt_raw[0].T
    bias, alog, skips = dt_bias[None], a_log[None], skip[None]
    hin, gin, *prepared = edges(x, y, bc, dt, bias, alog)
    grad_x, grad_bc, grad_dt, sums = main(y, dt, bias, alog, skips, hin, gin, *prepared)
    return (grad_x[None], grad_bc[None], grad_dt.T[None], sums)


def solution(mesh):
    placed = (
        P("dp", "seq", "head"),
        P("dp", "seq", None),
        P("dp", "seq", "head"),
        P("dp", "seq", "head"),
        P("head"),
        P("head"),
        P("head"),
    )
    return jax.shard_map(
        shards,
        mesh=mesh,
        in_specs=placed,
        out_specs=(
            P("dp", "seq", "head"),
            P("dp", "seq", None),
            P("dp", "seq", "head"),
            P(None, "head"),
        ),
        check_vma=False,
    )
```

```python
import functools
import math

import jax
import jax.numpy as jnp
from jax import lax
from jax.experimental import pallas as pl
from jax.experimental.pallas import tpu as pltpu
from jax.sharding import PartitionSpec as P

Q = 64
LAG = 2
CHUNK = 256
HEADDIM = 64
LANES = 128
HIGH = lax.Precision.HIGHEST
F32 = jnp.float32
BF16 = jnp.bfloat16
VMEM_LIMIT = 60 * 1024 * 1024


def dot_nn(a, b, precision=None):
    return lax.dot_general(a, b, (((1,), (0,)), ((), ())), precision=precision, preferred_element_type=F32)


def dot_nt(a, b):
    return lax.dot_general(a, b, (((1,), (1,)), ((), ())), preferred_element_type=F32)


def halves(value):
    hi = value.astype(BF16)
    return hi, (value - hi.astype(F32)).astype(BF16)


def iota(shape, dim):
    return lax.broadcasted_iota(jnp.int32, shape, dim)


def triangle(upper):
    r, c = iota((Q, Q), 0), iota((Q, Q), 1)
    return jnp.where(r <= c if upper else r >= c, 1.0, 0.0).astype(F32)


def repeat_heads(value, heads):
    pick = jnp.where(iota((heads, LANES), 1) % heads == iota((heads, LANES), 0), 1.0, 0.0)
    return dot_nn(value, pick.astype(F32), HIGH)


def packed(value, heads, terms):
    lane = iota(value.shape, 1)
    total = jnp.zeros_like(value)
    rest = value
    for term in range(terms):
        part = rest.astype(BF16).astype(F32)
        total = jnp.where((lane >= term * heads) & (lane < (term + 1) * heads), part, total)
        rest = rest - part
    return total.astype(BF16)


def head_lanes(heads, width):
    shape = (LANES, width)
    return jnp.where(iota(shape, 0) % heads == iota(shape, 1) // HEADDIM, 1.0, 0.0).astype(BF16)


def steps_of(dt_ref, bias_ref, heads):
    turned = jnp.transpose(jnp.concatenate([dt_ref[...]] * (LANES // heads), axis=0))
    return turned + repeat_heads(jnp.broadcast_to(bias_ref[...], (8, heads)), heads)[:1]


def rates_of(alog_ref, heads):
    return -jnp.exp(repeat_heads(jnp.broadcast_to(alog_ref[...], (8, heads)), heads))[:1]


def edges_kernel(heads, x_ref, y_ref, bc_ref, dt_ref, bias_ref, alog_ref, weight_ref,
                 gin_ref, hst, skip_ref, part, dts, shs, rows, vs, xo_ref, lo_ref, fo_ref, ab_ref,
                 pe, pf, le, lf, bt, ct, sel, xb, yb, xs, dec, mine, out0, got0, chip, gath, pre, inc, fin,
                 xbuf, lbuf, fbuf, abuf, bbuf, yx, hz, prods,
                 load_sem, s0, r0, s1, r1, s2, r2, s3, r3, put_sem, put_one):
    length = bc_ref.shape[0]
    blocks = length // Q
    groups = gin_ref.shape[0]
    state = gin_ref.shape[1]
    me = lax.axis_index("seq")
    core = lax.rem(me, 2)
    place = me // 2
    ahead = core == 1
    behind = core == 0
    partner = me + 1 - 2 * core

    def peer(d):
        return lax.rem(place + d, groups)

    def loads(i):
        g = peer(1 + i)
        span = pl.ds(pl.multiple_of(g * CHUNK, CHUNK), CHUNK)
        return (pltpu.make_async_copy(x_ref.at[:, span], xb.at[i], load_sem.at[0, i]),
                pltpu.make_async_copy(y_ref.at[:, span], yb.at[i], load_sem.at[1, i]))

    def swap(i):
        return pltpu.make_async_remote_copy(
            src_ref=out0.at[i], dst_ref=got0.at[i], send_sem=s0.at[i], recv_sem=r0.at[i],
            device_id={"seq": partner}, device_id_type=pl.DeviceIdType.MESH)

    def spread(d):
        return pltpu.make_async_remote_copy(
            src_ref=chip.at[d - 1], dst_ref=gath.at[place], send_sem=s1.at[d - 1], recv_sem=r1.at[place],
            device_id={"seq": peer(d) * 2 + core}, device_id_type=pl.DeviceIdType.MESH)

    def spread_in(source):
        return pltpu.make_async_remote_copy(
            src_ref=chip.at[0], dst_ref=gath.at[source], send_sem=s1.at[0], recv_sem=r1.at[source],
            device_id={"seq": source * 2 + core}, device_id_type=pl.DeviceIdType.MESH)

    def back(pos):
        return pltpu.make_async_remote_copy(
            src_ref=pre.at[pos], dst_ref=inc.at[place], send_sem=s2.at[pos], recv_sem=r2.at[place],
            device_id={"seq": pos * 2 + core}, device_id_type=pl.DeviceIdType.MESH)

    def back_in(source):
        return pltpu.make_async_remote_copy(
            src_ref=pre.at[source], dst_ref=inc.at[source], send_sem=s2.at[source], recv_sem=r2.at[source],
            device_id={"seq": source * 2 + core}, device_id_type=pl.DeviceIdType.MESH)

    def hand(g):
        return pltpu.make_async_remote_copy(
            src_ref=inc.at[g], dst_ref=fin.at[g], send_sem=s3.at[g], recv_sem=r3.at[g],
            device_id={"seq": partner}, device_id_type=pl.DeviceIdType.MESH)

    for i in range(groups):
        for copy in loads(i):
            copy.start()
    barrier = pltpu.get_barrier_semaphore()
    pl.semaphore_signal(barrier, inc=1, device_id={"seq": partner}, device_id_type=pl.DeviceIdType.MESH)
    for d in range(1, groups):
        pl.semaphore_signal(barrier, inc=1, device_id={"seq": peer(d) * 2 + core}, device_id_type=pl.DeviceIdType.MESH)

    sel[...] = head_lanes(heads, sel.shape[1])
    rate = rates_of(alog_ref, heads)
    shifted = steps_of(dt_ref, bias_ref, heads)
    shs[...] = shifted
    dt = jax.nn.softplus(shifted)
    dts[...] = dt
    tri = triangle(False)
    cums = [dot_nn(tri, dt[k * Q:(k + 1) * Q] * rate, HIGH) for k in range(blocks)]
    before = jnp.zeros((1, LANES), F32)
    for k in range(blocks):
        mid = cums[k][Q // 2 - 1:Q // 2]
        le[pl.ds(k * Q, Q), :] = packed(jnp.exp(cums[k] - mid), heads, 2)
        lf[pl.ds(k * Q, Q), :] = packed(dt[k * Q:(k + 1) * Q] * jnp.exp(mid - cums[k]), heads, 2)
        pe[pl.ds(k * Q, Q), :] = packed(jnp.exp(cums[k] + before), heads, 2)
        before = before + cums[k][Q - 1:Q]
    after = jnp.zeros((1, LANES), F32)
    for k in reversed(range(blocks)):
        last = cums[k][Q - 1:Q]
        pf[pl.ds(k * Q, Q), :] = packed(dt[k * Q:(k + 1) * Q] * jnp.exp((last - cums[k]) + after), heads, 2)
        after = after + last
    dec[...] = packed(jnp.broadcast_to(jnp.exp(before), (8, LANES)), heads, 3)
    b_t = jnp.transpose(bc_ref[:, :LANES].astype(F32)).astype(BF16)
    c_t = jnp.transpose(bc_ref[:, LANES:].astype(F32)).astype(BF16)
    bt[:, :length] = b_t
    bt[:, length:] = b_t
    ct[:, :length] = c_t
    ct[:, length:] = c_t
    pl.semaphore_wait(barrier, groups)

    def combine(i):
        swap(i).wait_recv()
        keep = out0[i, state:state + 1, :]
        value = mine[i] + keep * got0[i, :state, :]
        decay = out0[i, state:, :] * got0[i, state:, :]
        if i < groups - 1:
            chip[i, :state, :] = value
            chip[i, state:, :] = decay

            @pl.when(ahead)
            def _():
                spread(i + 1).start()
        else:
            gath[place, :state, :] = value
            gath[place, state:, :] = decay

    for i in range(groups):
        g = peer(1 + i)
        here = sel[:, pl.ds(pl.multiple_of(g * CHUNK, CHUNK), CHUNK)]
        copy_x, copy_y = loads(i)
        copy_x.wait()
        hi, lo = halves(dot_nn(pf[...], here) * xb[i].astype(F32))
        xs[:length] = hi
        xs[length:] = lo
        ends = dot_nn(bt[...], xs[...])
        copy_y.wait()
        hi, lo = halves(dot_nn(pe[...], here) * yb[i].astype(F32))
        xs[:length] = hi
        xs[length:] = lo
        starts = dot_nn(ct[...], xs[...])
        mine[i] = jnp.where(ahead, ends, starts)
        out0[i, :state, :] = jnp.where(ahead, starts, ends)
        out0[i, state:, :] = dot_nn(dec[...], here)
        swap(i).start()
        if i:
            combine(i - 1)
    combine(groups - 1)

    def scan():
        total = jnp.zeros((state, CHUNK), F32)
        for d in range(1, groups):
            spread_in(peer(d)).wait_recv()
        for k in range(groups):
            pos = jnp.where(ahead, k, groups - 1 - k)

            @pl.when(pos == place)
            def _():
                inc[place] = total

            @pl.when(pos != place)
            def _():
                pre[pos] = total
                back(pos).start()

            total = gath[pos, state:state + 1, :] * total + gath[pos, :state, :]

    def puts(i):
        g = peer(1 + i)
        span = pl.ds(pl.multiple_of(g * CHUNK, CHUNK), CHUNK)
        return (pltpu.make_async_copy(xbuf.at[:, :, span], xo_ref.at[:, :, span], put_sem.at[0, i]),
                pltpu.make_async_copy(lbuf.at[:, :, span], lo_ref.at[:, :, span], put_sem.at[1, i]),
                pltpu.make_async_copy(fbuf.at[:, span], fo_ref.at[:, span], put_sem.at[2, i]))

    for i in range(groups):
        g = peer(1 + i)
        span = pl.ds(pl.multiple_of(g * CHUNK, CHUNK), CHUNK)
        here = sel[:, span]
        x = xb[i].astype(F32)
        y = yb[i].astype(F32)
        f = dot_nn(lf[...], here)
        fbuf[:, span] = f
        hi, lo = halves(f * x)
        xbuf[:, :Q, span] = lo.reshape(blocks, Q, CHUNK)
        xbuf[:, Q:, span] = hi.reshape(blocks, Q, CHUNK)
        hi, lo = halves(dot_nn(le[...], here) * y)
        lbuf[:, :Q, span] = lo.reshape(blocks, Q, CHUNK)
        lbuf[:, Q:, span] = hi.reshape(blocks, Q, CHUNK)
        yx[:, span] = jnp.sum((y * x).reshape(length // 8, 8, CHUNK), axis=0)
        for copy in puts(i):
            copy.start()
        if i == groups // 2:
            pl.when(ahead)(scan)

    def hand_all():
        for d in range(groups):
            g = peer(d)
            if d:
                back_in(g).wait_recv()
            hand(g).start()

    def spread_all():
        for d in range(1, groups):
            spread(d).start()

    gone = jnp.concatenate([jnp.exp(cum[Q - 1:Q] - cum[Q // 2 - 1:Q // 2]) for cum in cums], axis=0)
    come = jnp.concatenate([jnp.exp(cum[Q // 2 - 1:Q // 2]) for cum in cums], axis=0)
    weights = repeat_heads(jnp.broadcast_to(weight_ref[...], (8, heads)), heads)
    rows[...] = dot_nn(packed(jnp.concatenate([gone, come, weights], axis=0), heads, 3), sel[...])

    lane = iota((Q, 2 * Q), 1)
    row = iota((Q, 2 * Q), 0)
    none = jnp.zeros((Q, 2 * Q), F32)

    @pl.loop(0, blocks)
    def _(k):
        span = pl.ds(pl.multiple_of(k * Q, Q), Q)
        b, c = bc_ref[span, :LANES], bc_ref[span, LANES:]
        bb = jnp.concatenate([b, b], axis=0)
        cc = jnp.concatenate([c, c], axis=0)
        lower = row >= lane % Q
        for dest, one, two, keep in ((abuf, c, bb, lower), (bbuf, b, cc, row <= lane % Q)):
            s_hi, s_lo = halves(jnp.where(keep, dot_nt(one, two), none))
            dest[k, :Q, :2 * Q] = one
            dest[k, :Q, 2 * Q:] = s_hi
            dest[k, Q:3 * Q, :2 * Q] = jnp.zeros((2 * Q, 2 * Q), BF16)
            dest[k, Q:3 * Q, 2 * Q:] = jnp.transpose(two.astype(F32)).astype(BF16)
            dest[k, 3 * Q:, :2 * Q] = s_lo
            dest[k, 3 * Q:, 2 * Q:] = one
        r = dot_nt(lbuf[k], xbuf[k])
        pair = jnp.where(lower, r[:Q] + r[Q:], none)
        p_hi, p_lo = halves(pair)
        part[span, LANES:] = dot_nn(p_hi, bb) + dot_nn(p_lo, bb)
        turned = jnp.transpose(pair)
        t_hi, t_lo = halves(turned[:Q] + turned[Q:])
        part[span, :LANES] = dot_nn(t_hi, c) + dot_nn(t_lo, c)

        @pl.when((k == blocks // 4) & behind)
        def _():
            spread_all()

        @pl.when((k == blocks // 2) & ahead)
        def _():
            hand_all()

    put_ab = pltpu.make_async_copy(bbuf, ab_ref, put_one)
    put_ab.start()
    sums = jnp.sum(yx[...], axis=0, keepdims=True)
    hi, lo = halves(jnp.broadcast_to(sums, yx.shape))
    skip_ref[...] = dot_nt(hi, sel[...]) + dot_nt(lo, sel[...])

    def own(d):
        g = peer(d)
        i = (d - 1) % groups
        return got0[i, state:state + 1, :] * inc[g] + got0[i, :state, :]

    def lanes_of(d):
        return pl.ds(pl.multiple_of(peer(d) * CHUNK, CHUNK), CHUNK)

    @pl.when(ahead)
    def _():
        for d in range(groups):
            hst[:, lanes_of(d)] = own(d)

    @pl.when(behind)
    def _():
        for d in range(groups):
            hand(peer(d)).wait_recv()
            hst[:, lanes_of(d)] = fin[peer(d)]

    chunks = [slice(c * CHUNK, (c + 1) * CHUNK) for c in range(groups)]
    for c in chunks:
        h = hst[:, c] * rows[blocks:blocks + 1, c]
        hst[:, c] = h
        hz[0, :128, c], hz[0, 128:, c] = halves(h)

    @pl.loop(0, blocks)
    def _(k):
        span = pl.ds(pl.multiple_of(k * Q, Q), Q)
        now = lax.rem(k, 2)
        first, second = abuf[k, :192], abuf[k, 192:]
        come = blocks + jnp.minimum(k + 1, blocks - 1)
        for c in chunks:
            wide = xbuf[k, :, c]
            one = dot_nn(first, jnp.concatenate([hz[now, :128, c], wide], axis=0))
            two = dot_nn(second, jnp.concatenate([wide, hz[now, 128:, c]], axis=0))
            lifted = lbuf[k, 64:, c].astype(F32) + lbuf[k, :64, c].astype(F32)
            prods[0:64, c], prods[64:128, c] = halves(lifted * (one[:64] + two))
            h = (hst[:, c] + one[64:]) * rows[pl.ds(k, 1), c]
            h = h * jnp.where(k == blocks - 1, 1.0, rows[pl.ds(come, 1), c])
            hst[:, c] = h
            hz[1 - now, :128, c], hz[1 - now, 128:, c] = halves(h)
        sums = dot_nt(prods[...], sel[...])
        vs[span, :] = sums[0:64] + sums[64:128]
        r = dot_nt(hz[now], lbuf[k])
        turned = jnp.transpose(r[:128] + r[128:])
        part[span, LANES:] += turned[:64] + turned[64:]

        @pl.when((k == blocks // 4) & behind)
        def _():
            scan()

        @pl.when((k == 3 * blocks // 4) & behind)
        def _():
            hand_all()

    @pl.when(ahead)
    def _():
        for d in range(groups):
            hand(peer(d)).wait_recv()
            gin_ref[peer(d)] = fin[peer(d)]

    @pl.when(behind)
    def _():
        for d in range(groups):
            gin_ref[peer(d)] = own(d)

    for i in range(groups):
        swap(i).wait_send()
        hand(i).wait_send()
    for d in range(1, groups):
        spread(d).wait_send()
        back(peer(d)).wait_send()
    for i in range(groups):
        for copy in puts(i):
            copy.wait()
    put_ab.wait()


def edges(x, y, bc, dt, bias, alog, skip):
    length, width = x.shape
    heads = dt.shape[0]
    state = bc.shape[1] // 2
    groups = width // CHUNK
    blocks = length // Q
    whole = pl.BlockSpec(memory_space=pltpu.VMEM)
    anywhere = pl.BlockSpec(memory_space=pl.ANY)
    dma = pltpu.SemaphoreType.DMA
    return pl.pallas_call(
        functools.partial(edges_kernel, heads),
        out_shape=(
            jax.ShapeDtypeStruct((groups, state, CHUNK), F32),
            jax.ShapeDtypeStruct((state, width), F32),
            jax.ShapeDtypeStruct((8, LANES), F32),
            jax.ShapeDtypeStruct((length, 2 * state), F32),
            jax.ShapeDtypeStruct((length, LANES), F32),
            jax.ShapeDtypeStruct((length, LANES), F32),
            jax.ShapeDtypeStruct((2 * blocks + 8, width), F32),
            jax.ShapeDtypeStruct((length, LANES), F32),
            jax.ShapeDtypeStruct((blocks, 2 * Q, width), BF16),
            jax.ShapeDtypeStruct((blocks, 2 * Q, width), BF16),
            jax.ShapeDtypeStruct((length, width), F32),
            jax.ShapeDtypeStruct((blocks, 4 * Q, 4 * Q), BF16),
        ),
        in_specs=[anywhere, anywhere] + [whole] * 5,
        out_specs=(whole,) * 8 + (anywhere,) * 4,
        scratch_shapes=[
            pltpu.VMEM((length, LANES), BF16),
            pltpu.VMEM((length, LANES), BF16),
            pltpu.VMEM((length, LANES), BF16),
            pltpu.VMEM((length, LANES), BF16),
            pltpu.VMEM((state, 2 * length), BF16),
            pltpu.VMEM((state, 2 * length), BF16),
            pltpu.VMEM((LANES, width), BF16),
            pltpu.VMEM((groups, length, CHUNK), BF16),
            pltpu.VMEM((groups, length, CHUNK), BF16),
            pltpu.VMEM((2 * length, CHUNK), BF16),
            pltpu.VMEM((8, LANES), BF16),
            pltpu.VMEM((groups, state, CHUNK), F32),
            pltpu.VMEM((groups, state + 8, CHUNK), F32),
            pltpu.VMEM((groups, state + 8, CHUNK), F32),
            pltpu.VMEM((groups - 1, state + 8, CHUNK), F32),
            pltpu.VMEM((groups, state + 8, CHUNK), F32),
            pltpu.VMEM((groups, state, CHUNK), F32),
            pltpu.VMEM((groups, state, CHUNK), F32),
            pltpu.VMEM((groups, state, CHUNK), F32),
            pltpu.VMEM((blocks, 2 * Q, width), BF16),
            pltpu.VMEM((blocks, 2 * Q, width), BF16),
            pltpu.VMEM((length, width), F32),
            pltpu.VMEM((blocks, 4 * Q, 4 * Q), BF16),
            pltpu.VMEM((blocks, 4 * Q, 4 * Q), BF16),
            pltpu.VMEM((8, width), F32),
            pltpu.VMEM((2, 256, width), BF16),
            pltpu.VMEM((128, width), BF16),
            dma((2, groups)),
            dma((groups,)), dma((groups,)),
            dma((groups,)), dma((groups,)),
            dma((groups,)), dma((groups,)),
            dma((groups,)), dma((groups,)),
            dma((3, groups)), dma,
        ],
        compiler_params=pltpu.CompilerParams(vmem_limit_bytes=VMEM_LIMIT, collective_id=0, has_side_effects=True),
        cost_estimate=pl.CostEstimate(flops=8 * length * width * state, bytes_accessed=4 * length * width, transcendentals=0),
    )(x, y, bc, dt, bias, alog, skip)


def main_kernel(heads, zs, dps, flats, scale, xb_ref, lb_ref, fb_ref, yb_ref, ab_ref,
                gin_ref, hend_ref, dskip_ref, part_ref, dts, shs, rows, vs, alog_ref,
                gx_ref, gbc_ref, gdt_ref, gheads_ref,
                sel, ws, gz, prods, gst,
                stage, landed, done, hsum, hgot, s1, r1s, s2, r2s, s3, r3s):
    length = dts.shape[0]
    width = sel.shape[1]
    blocks = length // Q
    step = pl.program_id(0)
    kb = blocks - 1 - step
    chunks = [slice(c * CHUNK, (c + 1) * CHUNK) for c in range(width // CHUNK)]
    rate = rates_of(alog_ref, heads)
    lines = Q // zs
    z = lax.axis_index("head")
    flat = lax.axis_index("seq") * dps + lax.axis_index("dp")
    barrier = pltpu.get_barrier_semaphore()

    def zpeer(d):
        return {"head": lax.rem(z + d, zs)}

    def fpeer(d):
        other = lax.rem(flat + d, flats)
        return {"seq": other // dps, "dp": lax.rem(other, dps)}

    def scatter(j, d):
        q = lax.rem(z + d, zs)
        return pltpu.make_async_remote_copy(
            src_ref=stage.at[j, q], dst_ref=landed.at[j, z], send_sem=s1.at[j, q], recv_sem=r1s.at[j, z],
            device_id=zpeer(d), device_id_type=pl.DeviceIdType.MESH)

    def scatter_in(j, d):
        q = lax.rem(z + d, zs)
        return pltpu.make_async_remote_copy(
            src_ref=stage.at[j, q], dst_ref=landed.at[j, q], send_sem=s1.at[j, q], recv_sem=r1s.at[j, q],
            device_id=zpeer(d), device_id_type=pl.DeviceIdType.MESH)

    def gather(j, d):
        q = lax.rem(z + d, zs)
        return pltpu.make_async_remote_copy(
            src_ref=done.at[j, z], dst_ref=done.at[j, z], send_sem=s2.at[j, q], recv_sem=r2s.at[j, z],
            device_id=zpeer(d), device_id_type=pl.DeviceIdType.MESH)

    def gather_in(j, d):
        q = lax.rem(z + d, zs)
        return pltpu.make_async_remote_copy(
            src_ref=done.at[j, q], dst_ref=done.at[j, q], send_sem=s2.at[j, q], recv_sem=r2s.at[j, q],
            device_id=zpeer(d), device_id_type=pl.DeviceIdType.MESH)

    def share(d):
        return pltpu.make_async_remote_copy(
            src_ref=hsum, dst_ref=hgot.at[flat], send_sem=s3.at[d], recv_sem=r3s.at[flat],
            device_id=fpeer(d), device_id_type=pl.DeviceIdType.MESH)

    def share_in(d):
        other = lax.rem(flat + d, flats)
        return pltpu.make_async_remote_copy(
            src_ref=hsum, dst_ref=hgot.at[other], send_sem=s3.at[d], recv_sem=r3s.at[other],
            device_id=fpeer(d), device_id_type=pl.DeviceIdType.MESH)

    def reduce_pair(j):
        for d in range(1, zs):
            scatter_in(j, d).wait_recv()
        landed[j, z] = stage[j, z]
        total = landed[j, 0]
        for q in range(1, zs):
            total = total + landed[j, q]
        done[j, z] = total
        for d in range(1, zs):
            gather(j, d).start()

    def finish_pair(j):
        for d in range(1, zs):
            gather_in(j, d).wait_recv()
        for q in range(zs):
            gbc_ref[pl.ds(pl.multiple_of((blocks - 1 - j) * Q + q * lines, lines), lines), LANES:] = done[j, q, :lines]
            gbc_ref[pl.ds(pl.multiple_of((blocks - 1 - j) * Q + q * lines, lines), lines), :LANES] = done[j, q, lines:]

    @pl.when(step == 0)
    def _():
        for d in range(1, zs):
            pl.semaphore_signal(barrier, inc=1, device_id=zpeer(d), device_id_type=pl.DeviceIdType.MESH)

        @pl.loop(1, flats)
        def _(d):
            pl.semaphore_signal(barrier, inc=1, device_id=fpeer(d), device_id_type=pl.DeviceIdType.MESH)

        sel[...] = head_lanes(heads, width)
        for i, c in enumerate(chunks):
            g = gin_ref[i] * rows[blocks - 1:blocks, c]
            gst[:, c] = g
            gz[0, :128, c], gz[0, 128:, c] = halves(g)

    span = pl.ds(pl.multiple_of(kb * Q, Q), Q)
    now = lax.rem(step, 2)
    first, second = ab_ref[0, :192], ab_ref[0, 192:]
    come = jnp.maximum(kb - 1, 0)
    for c in chunks:
        wide = lb_ref[0, :, c]
        one = dot_nn(first, jnp.concatenate([gz[now, :128, c], wide], axis=0))
        two = dot_nn(second, jnp.concatenate([wide, gz[now, 128:, c]], axis=0))
        out = one[:64] + two
        xs = xb_ref[0, 64:, c].astype(F32) + xb_ref[0, :64, c].astype(F32)
        prods[0:64, c], prods[64:128, c] = halves(xs * out)
        gx_ref[:, c] = (fb_ref[:, c] * out + rows[2 * blocks:2 * blocks + 1, c] * yb_ref[:, c].astype(F32)).astype(BF16)
        g = (gst[:, c] + one[64:]) * rows[pl.ds(blocks + kb, 1), c] * rows[pl.ds(come, 1), c]
        gst[:, c] = g
        gz[1 - now, :128, c], gz[1 - now, 128:, c] = halves(g)

    sums = dot_nt(prods[...], sel[...])
    ws[span, :] = sums[0:64] + sums[64:128]
    r = dot_nt(gz[now], xb_ref[0])
    turned = jnp.transpose(r[:128] + r[128:])
    grad_b = part_ref[span, :LANES] + turned[:64] + turned[64:]
    grad_c = part_ref[span, LANES:]
    stage[step, :, :lines] = grad_c.reshape(zs, lines, LANES)
    stage[step, :, lines:] = grad_b.reshape(zs, lines, LANES)

    @pl.when(step == 0)
    def _():
        pl.semaphore_wait(barrier, zs - 1 + flats - 1)

    for d in range(1, zs):
        scatter(step, d).start()

    @pl.when(step >= LAG)
    def _():
        reduce_pair(step - LAG)

    @pl.when(step >= 2 * LAG)
    def _():
        finish_pair(step - 2 * LAG)

    @pl.when(step == blocks - 1)
    def _():
        closing = jnp.concatenate(
            [jnp.sum(gin_ref[i] * hend_ref[:, c], axis=0, keepdims=True) for i, c in enumerate(chunks)], axis=1)
        hi, lo = halves(jnp.broadcast_to(closing, (16, width)))
        totals = dot_nt(hi, sel[...]) + dot_nt(lo, sel[...])
        after = totals[0:1]
        gdts = []
        tri = triangle(True)
        d_alog = jnp.zeros((1, LANES), F32)
        d_bias = jnp.zeros((1, LANES), F32)
        for k in reversed(range(blocks)):
            span = slice(k * Q, (k + 1) * Q)
            w = ws[span]
            dt = dts[span]
            dlog = dot_nn(tri, vs[span] - w, HIGH) + after
            after = dlog[0:1]
            grad_dt = (w / dt + dlog * rate) * jax.nn.sigmoid(shs[span])
            gdts.append(grad_dt)
            d_alog = d_alog + jnp.sum(dlog * dt, axis=0, keepdims=True)
            d_bias = d_bias + jnp.sum(grad_dt, axis=0, keepdims=True)
        hsum[...] = jnp.concatenate([d_alog * rate, d_bias, dskip_ref[0:1], jnp.zeros((5, LANES), F32)], axis=0)

        @pl.loop(1, flats)
        def _(d):
            share(d).start()

        for j in range(blocks - LAG, blocks):
            reduce_pair(j)
        gdt_ref[...] = jnp.transpose(jnp.concatenate(gdts[::-1], axis=0))[:heads]
        for j in range(blocks - 2 * LAG, blocks - LAG):
            finish_pair(j)
        hgot[flat] = hsum[...]

        @pl.loop(1, flats)
        def _(d):
            share_in(d).wait_recv()

        total = hgot[0]
        for other in range(1, flats):
            total = total + hgot[other]
        gheads_ref[...] = total[:3, :heads] * scale
        for j in range(blocks - LAG, blocks):
            finish_pair(j)

        @pl.loop(1, flats)
        def _(d):
            share(d).wait_send()

        @pl.loop(0, blocks)
        def _(j):
            for d in range(1, zs):
                scatter(j, d).wait_send()
                gather(j, d).wait_send()


def main(heads, y, alog, gin, hend, dskip, part, dts, shs, rows, vs, xs, ls, fs, ab):
    length, width = y.shape
    state = gin.shape[1]
    blocks = length // Q
    zs, dps = lax.axis_size("head"), lax.axis_size("dp")
    flats = lax.axis_size("seq") * dps
    scale = 1.0 / math.sqrt(flats * length)
    lines = Q // zs
    dma = pltpu.SemaphoreType.DMA
    whole = pl.BlockSpec(memory_space=pltpu.VMEM)
    back = pl.BlockSpec((Q, width), lambda i: (blocks - 1 - i, 0))
    pair_b = pl.BlockSpec((1, 2 * Q, width), lambda i: (blocks - 1 - i, 0, 0))
    left_b = pl.BlockSpec((1, 4 * Q, 4 * Q), lambda i: (blocks - 1 - i, 0, 0))
    return pl.pallas_call(
        functools.partial(main_kernel, heads, zs, dps, flats, scale),
        grid=(blocks,),
        out_shape=(
            jax.ShapeDtypeStruct((length, width), BF16),
            jax.ShapeDtypeStruct((length, 2 * state), F32),
            jax.ShapeDtypeStruct((heads, length), F32),
            jax.ShapeDtypeStruct((3, heads), F32),
        ),
        in_specs=[pair_b, pair_b, back, back, left_b] + [whole] * 9,
        out_specs=(back, whole, whole, whole),
        scratch_shapes=[
            pltpu.VMEM((LANES, width), BF16),
            pltpu.VMEM((length, LANES), F32),
            pltpu.VMEM((2, 256, width), BF16),
            pltpu.VMEM((128, width), BF16),
            pltpu.VMEM((state, width), F32),
            pltpu.VMEM((blocks, zs, 2 * lines, state), F32),
            pltpu.VMEM((blocks, zs, 2 * lines, state), F32),
            pltpu.VMEM((blocks, zs, 2 * lines, state), F32),
            pltpu.VMEM((8, LANES), F32),
            pltpu.VMEM((flats, 8, LANES), F32),
            dma((blocks, zs)), dma((blocks, zs)),
            dma((blocks, zs)), dma((blocks, zs)),
            dma((flats,)), dma((flats,)),
        ],
        compiler_params=pltpu.CompilerParams(
            vmem_limit_bytes=VMEM_LIMIT, collective_id=1, has_side_effects=True, dimension_semantics=("arbitrary",)),
        cost_estimate=pl.CostEstimate(flops=60 * length * width * state, bytes_accessed=12 * length * width, transcendentals=0),
    )(xs, ls, fs, y, ab, gin, hend, dskip, part, dts, shs, rows, vs, alog)


def shards(inputs_x, inputs_bc, dt_raw, grad_out, a_log, dt_bias, skip):
    heads = a_log.shape[0]
    x, y, bc, dt = inputs_x[0], grad_out[0], inputs_bc[0], dt_raw[0].T
    bias, alog, skips = dt_bias[None], a_log[None], skip[None]
    prepared = edges(x, y, bc, dt, bias, alog, skips)
    grad_x, grad_bc, grad_dt, sums = main(heads, y, alog, *prepared)
    return (grad_x[None], grad_bc[None], grad_dt.T[None], sums)


def solution(mesh):
    placed = (
        P("dp", "seq", "head"),
        P("dp", "seq", None),
        P("dp", "seq", "head"),
        P("dp", "seq", "head"),
        P("head"),
        P("head"),
        P("head"),
    )
    return jax.shard_map(
        shards,
        mesh=mesh,
        in_specs=placed,
        out_specs=(
            P("dp", "seq", "head"),
            P("dp", "seq", None),
            P("dp", "seq", "head"),
            P(None, "head"),
        ),
        check_vma=False,
    )
```

```python
import functools
import math

import jax
import jax.numpy as jnp
from jax import lax
from jax.experimental import pallas as pl
from jax.experimental.pallas import tpu as pltpu
from jax.sharding import PartitionSpec as P

Q = 64
LAG = 3
CHUNK = 256
HEADDIM = 64
LANES = 128
HIGH = lax.Precision.HIGHEST
F32 = jnp.float32
BF16 = jnp.bfloat16
VMEM_LIMIT = 60 * 1024 * 1024


def dot_nn(a, b, precision=None):
    return lax.dot_general(a, b, (((1,), (0,)), ((), ())), precision=precision, preferred_element_type=F32)


def dot_nt(a, b):
    return lax.dot_general(a, b, (((1,), (1,)), ((), ())), preferred_element_type=F32)


def halves(value):
    hi = value.astype(BF16)
    return hi, (value - hi.astype(F32)).astype(BF16)


def iota(shape, dim):
    return lax.broadcasted_iota(jnp.int32, shape, dim)


def triangle(upper):
    r, c = iota((Q, Q), 0), iota((Q, Q), 1)
    return jnp.where(r <= c if upper else r >= c, 1.0, 0.0).astype(F32)


def repeat_heads(value, heads):
    pick = jnp.where(iota((heads, LANES), 1) % heads == iota((heads, LANES), 0), 1.0, 0.0)
    return dot_nn(value, pick.astype(F32), HIGH)


def packed(value, heads, terms):
    lane = iota(value.shape, 1)
    total = jnp.zeros_like(value)
    rest = value
    for term in range(terms):
        part = rest.astype(BF16).astype(F32)
        total = jnp.where((lane >= term * heads) & (lane < (term + 1) * heads), part, total)
        rest = rest - part
    return total.astype(BF16)


def head_lanes(heads, width):
    shape = (LANES, width)
    return jnp.where(iota(shape, 0) % heads == iota(shape, 1) // HEADDIM, 1.0, 0.0).astype(BF16)


def steps_of(dt_ref, bias_ref, heads):
    turned = jnp.transpose(jnp.concatenate([dt_ref[...]] * (LANES // heads), axis=0))
    return turned + repeat_heads(jnp.broadcast_to(bias_ref[...], (8, heads)), heads)[:1]


def rates_of(alog_ref, heads):
    return -jnp.exp(repeat_heads(jnp.broadcast_to(alog_ref[...], (8, heads)), heads))[:1]


class HeadSum:
    def __init__(self, stage, landed, done, sems):
        self.stage, self.landed, self.done = stage, landed, done
        self.s1, self.r1, self.s2, self.r2 = sems
        self.zs, self.z = stage.shape[1], lax.axis_index("head")

    def peer(self, d):
        return lax.rem(self.z + d, self.zs)

    def copy(self, src, dst, send, recv, q):
        return pltpu.make_async_remote_copy(
            src_ref=src, dst_ref=dst, send_sem=send, recv_sem=recv,
            device_id={"head": q}, device_id_type=pl.DeviceIdType.MESH)

    def scatter(self, j, d):
        q = self.peer(d)
        return self.copy(self.stage.at[j, q], self.landed.at[j, self.z], self.s1.at[j, q], self.r1.at[j, self.z], q)

    def gather(self, j, d):
        q = self.peer(d)
        return self.copy(self.done.at[j, self.z], self.done.at[j, self.z], self.s2.at[j, q], self.r2.at[j, self.z], q)

    def send(self, j, value):
        self.stage[j] = value.reshape(self.stage.shape[1:])
        for d in range(1, self.zs):
            self.scatter(j, d).start()

    def reduce(self, j):
        for d in range(1, self.zs):
            q = self.peer(d)
            self.copy(self.stage.at[j, q], self.landed.at[j, q], self.s1.at[j, q], self.r1.at[j, q], q).wait_recv()
        self.landed[j, self.z] = self.stage[j, self.z]
        total = self.landed[j, 0]
        for q in range(1, self.zs):
            total = total + self.landed[j, q]
        self.done[j, self.z] = total
        for d in range(1, self.zs):
            self.gather(j, d).start()

    def result(self, j):
        for d in range(1, self.zs):
            q = self.peer(d)
            self.copy(self.done.at[j, q], self.done.at[j, q], self.s2.at[j, q], self.r2.at[j, q], q).wait_recv()
        return self.done[j].reshape(Q, LANES)

    def sent(self):
        @pl.loop(0, self.stage.shape[0])
        def _(j):
            for d in range(1, self.zs):
                self.scatter(j, d).wait_send()
                self.gather(j, d).wait_send()


def head_sum_scratch(count, zs):
    buffer = pltpu.VMEM((count, zs, Q // zs, LANES), F32)
    return [buffer] * 3 + [pltpu.SemaphoreType.DMA((count, zs))] * 4


def greet_heads(barrier, zs):
    for d in range(1, zs):
        pl.semaphore_signal(barrier, inc=1, device_id={"head": lax.rem(lax.axis_index("head") + d, zs)},
                            device_id_type=pl.DeviceIdType.MESH)


def edges_kernel(heads, x_ref, y_ref, bc_ref, dt_ref, bias_ref, alog_ref, weight_ref,
                 gin_ref, hst, skip_ref, part, dts, shs, rows, vs, xo_ref, lo_ref, fo_ref, ab_ref,
                 pe, pf, le, lf, bt, ct, sel, xb, yb, xs, dec, out0, got0, chip, gath, pre, inc, fin,
                 xbuf, lbuf, fbuf, abuf, bbuf, yx, hz,
                 load_sem, s0, r0, s1, r1, s2, r2, s3, r3, put_sem, put_one,
                 stage, landed, done, z1, z2, z3, z4):
    length = bc_ref.shape[0]
    blocks = length // Q
    groups = gin_ref.shape[0]
    state = gin_ref.shape[1]
    me = lax.axis_index("seq")
    core = lax.rem(me, 2)
    place = me // 2
    ahead = core == 1
    behind = core == 0
    partner = me + 1 - 2 * core

    def peer(d):
        return lax.rem(place + d, groups)

    def loads(i):
        g = peer(1 + i)
        span = pl.ds(pl.multiple_of(g * CHUNK, CHUNK), CHUNK)
        return (pltpu.make_async_copy(x_ref.at[:, span], xb.at[i], load_sem.at[0, i]),
                pltpu.make_async_copy(y_ref.at[:, span], yb.at[i], load_sem.at[1, i]))

    def swap(i):
        return pltpu.make_async_remote_copy(
            src_ref=out0.at[i], dst_ref=got0.at[i], send_sem=s0.at[i], recv_sem=r0.at[i],
            device_id={"seq": partner}, device_id_type=pl.DeviceIdType.MESH)

    def spread(d):
        return pltpu.make_async_remote_copy(
            src_ref=chip.at[d - 1], dst_ref=gath.at[place], send_sem=s1.at[d - 1], recv_sem=r1.at[place],
            device_id={"seq": peer(d) * 2 + core}, device_id_type=pl.DeviceIdType.MESH)

    def spread_in(source):
        return pltpu.make_async_remote_copy(
            src_ref=chip.at[0], dst_ref=gath.at[source], send_sem=s1.at[0], recv_sem=r1.at[source],
            device_id={"seq": source * 2 + core}, device_id_type=pl.DeviceIdType.MESH)

    def back(pos):
        return pltpu.make_async_remote_copy(
            src_ref=pre.at[pos], dst_ref=inc.at[place], send_sem=s2.at[pos], recv_sem=r2.at[place],
            device_id={"seq": pos * 2 + core}, device_id_type=pl.DeviceIdType.MESH)

    def back_in(source):
        return pltpu.make_async_remote_copy(
            src_ref=pre.at[source], dst_ref=inc.at[source], send_sem=s2.at[source], recv_sem=r2.at[source],
            device_id={"seq": source * 2 + core}, device_id_type=pl.DeviceIdType.MESH)

    def hand(g):
        return pltpu.make_async_remote_copy(
            src_ref=inc.at[g], dst_ref=fin.at[g], send_sem=s3.at[g], recv_sem=r3.at[g],
            device_id={"seq": partner}, device_id_type=pl.DeviceIdType.MESH)

    for i in range(groups):
        for copy in loads(i):
            copy.start()
    total_c = HeadSum(stage, landed, done, (z1, z2, z3, z4))
    early = stage.shape[0]
    barrier = pltpu.get_barrier_semaphore()
    greet_heads(barrier, total_c.zs)
    pl.semaphore_signal(barrier, inc=1, device_id={"seq": partner}, device_id_type=pl.DeviceIdType.MESH)
    for d in range(1, groups):
        pl.semaphore_signal(barrier, inc=1, device_id={"seq": peer(d) * 2 + core}, device_id_type=pl.DeviceIdType.MESH)

    sel[...] = head_lanes(heads, sel.shape[1])
    rate = rates_of(alog_ref, heads)
    shifted = steps_of(dt_ref, bias_ref, heads)
    shs[...] = shifted
    dt = jax.nn.softplus(shifted)
    dts[...] = dt
    tri = triangle(False)
    cums = [dot_nn(tri, dt[k * Q:(k + 1) * Q] * rate, HIGH) for k in range(blocks)]
    before = jnp.zeros((1, LANES), F32)
    for k in range(blocks):
        mid = cums[k][Q // 2 - 1:Q // 2]
        le[pl.ds(k * Q, Q), :] = packed(jnp.exp(cums[k] - mid), heads, 2)
        lf[pl.ds(k * Q, Q), :] = packed(dt[k * Q:(k + 1) * Q] * jnp.exp(mid - cums[k]), heads, 2)
        pe[pl.ds(k * Q, Q), :] = packed(jnp.exp(cums[k] + before), heads, 2)
        before = before + cums[k][Q - 1:Q]
    after = jnp.zeros((1, LANES), F32)
    for k in reversed(range(blocks)):
        last = cums[k][Q - 1:Q]
        pf[pl.ds(k * Q, Q), :] = packed(dt[k * Q:(k + 1) * Q] * jnp.exp((last - cums[k]) + after), heads, 2)
        after = after + last
    dec[...] = packed(jnp.broadcast_to(jnp.exp(before), (8, LANES)), heads, 3)
    b_t = jnp.transpose(bc_ref[:, :LANES].astype(F32)).astype(BF16)
    c_t = jnp.transpose(bc_ref[:, LANES:].astype(F32)).astype(BF16)
    bt[:, :length] = b_t
    bt[:, length:] = b_t
    ct[:, :length] = c_t
    ct[:, length:] = c_t
    pl.semaphore_wait(barrier, groups + total_c.zs - 1)

    def combine(i):
        swap(i).wait_recv()
        keep = out0[i, state:state + 1, :]
        value = pre[i] + keep * got0[i, :state, :]
        decay = out0[i, state:, :] * got0[i, state:, :]
        if i < groups - 1:
            chip[i, :state, :] = value
            chip[i, state:, :] = decay

            @pl.when(ahead)
            def _():
                spread(i + 1).start()
        else:
            gath[place, :state, :] = value
            gath[place, state:, :] = decay

    for i in range(groups):
        g = peer(1 + i)
        here = sel[:, pl.ds(pl.multiple_of(g * CHUNK, CHUNK), CHUNK)]
        copy_x, copy_y = loads(i)
        copy_x.wait()
        hi, lo = halves(dot_nn(pf[...], here) * xb[i].astype(F32))
        xs[:length] = hi
        xs[length:] = lo
        ends = dot_nn(bt[...], xs[...])
        copy_y.wait()
        hi, lo = halves(dot_nn(pe[...], here) * yb[i].astype(F32))
        xs[:length] = hi
        xs[length:] = lo
        starts = dot_nn(ct[...], xs[...])
        pre[i] = jnp.where(ahead, ends, starts)
        out0[i, :state, :] = jnp.where(ahead, starts, ends)
        out0[i, state:, :] = dot_nn(dec[...], here)
        swap(i).start()
        if i:
            combine(i - 1)
    combine(groups - 1)

    def scan():
        total = jnp.zeros((state, CHUNK), F32)
        for d in range(1, groups):
            spread_in(peer(d)).wait_recv()
        for k in range(groups):
            pos = jnp.where(ahead, k, groups - 1 - k)

            @pl.when(pos == place)
            def _():
                inc[place] = total

            @pl.when(pos != place)
            def _():
                pre[pos] = total
                back(pos).start()

            total = gath[pos, state:state + 1, :] * total + gath[pos, :state, :]

    def puts(i):
        g = peer(1 + i)
        span = pl.ds(pl.multiple_of(g * CHUNK, CHUNK), CHUNK)
        return (pltpu.make_async_copy(xbuf.at[:, :, span], xo_ref.at[:, :, span], put_sem.at[0, i]),
                pltpu.make_async_copy(lbuf.at[:, :, span], lo_ref.at[:, :, span], put_sem.at[1, i]),
                pltpu.make_async_copy(fbuf.at[:, span], fo_ref.at[:, span], put_sem.at[2, i]))

    for i in range(groups):
        g = peer(1 + i)
        span = pl.ds(pl.multiple_of(g * CHUNK, CHUNK), CHUNK)
        here = sel[:, span]
        x = xb[i].astype(F32)
        y = yb[i].astype(F32)
        f = dot_nn(lf[...], here)
        fbuf[:, span] = f
        hi, lo = halves(f * x)
        xbuf[:, :Q, span] = lo.reshape(blocks, Q, CHUNK)
        xbuf[:, Q:, span] = hi.reshape(blocks, Q, CHUNK)
        hi, lo = halves(dot_nn(le[...], here) * y)
        lbuf[:, :Q, span] = lo.reshape(blocks, Q, CHUNK)
        lbuf[:, Q:, span] = hi.reshape(blocks, Q, CHUNK)
        yx[:, span] = jnp.sum((y * x).reshape(length // 8, 8, CHUNK), axis=0)
        for copy in puts(i):
            copy.start()
        if i == groups // 2:
            pl.when(ahead)(scan)

    def hand_all():
        for d in range(groups):
            g = peer(d)
            if d:
                back_in(g).wait_recv()
            hand(g).start()

    def spread_all():
        for d in range(1, groups):
            spread(d).start()

    gone = jnp.concatenate([jnp.exp(cum[Q - 1:Q] - cum[Q // 2 - 1:Q // 2]) for cum in cums], axis=0)
    come = jnp.concatenate([jnp.exp(cum[Q // 2 - 1:Q // 2]) for cum in cums], axis=0)
    weights = repeat_heads(jnp.broadcast_to(weight_ref[...], (8, heads)), heads)
    rows[...] = dot_nn(packed(jnp.concatenate([gone, come, weights], axis=0), heads, 3), sel[...])

    lane = iota((Q, 2 * Q), 1)
    row = iota((Q, 2 * Q), 0)
    none = jnp.zeros((Q, 2 * Q), F32)

    @pl.loop(0, blocks)
    def _(k):
        span = pl.ds(pl.multiple_of(k * Q, Q), Q)
        b, c = bc_ref[span, :LANES], bc_ref[span, LANES:]
        bb = jnp.concatenate([b, b], axis=0)
        cc = jnp.concatenate([c, c], axis=0)
        lower = row >= lane % Q
        for dest, one, two, keep in ((abuf, c, bb, lower), (bbuf, b, cc, row <= lane % Q)):
            s_hi, s_lo = halves(jnp.where(keep, dot_nt(one, two), none))
            dest[k, :Q, :2 * Q] = one
            dest[k, :Q, 2 * Q:] = s_hi
            dest[k, Q:3 * Q, :2 * Q] = jnp.zeros((2 * Q, 2 * Q), BF16)
            dest[k, Q:3 * Q, 2 * Q:] = jnp.transpose(two.astype(F32)).astype(BF16)
            dest[k, 3 * Q:, :2 * Q] = s_lo
            dest[k, 3 * Q:, 2 * Q:] = one
        r = dot_nt(lbuf[k], xbuf[k])
        pair = jnp.where(lower, r[:Q] + r[Q:], none)
        p_hi, p_lo = halves(pair)
        part[span, LANES:] = dot_nn(p_hi, bb) + dot_nn(p_lo, bb)
        turned = jnp.transpose(pair)
        t_hi, t_lo = halves(turned[:Q] + turned[Q:])
        part[span, :LANES] = dot_nn(t_hi, c) + dot_nn(t_lo, c)

        @pl.when((k == blocks // 4) & behind)
        def _():
            spread_all()

        @pl.when((k == blocks // 2) & ahead)
        def _():
            hand_all()

    put_ab = pltpu.make_async_copy(bbuf, ab_ref, put_one)
    put_ab.start()
    sums = jnp.sum(yx[...], axis=0, keepdims=True)
    hi, lo = halves(jnp.broadcast_to(sums, yx.shape))
    skip_ref[...] = dot_nt(hi, sel[...]) + dot_nt(lo, sel[...])

    def own(d):
        g = peer(d)
        i = (d - 1) % groups
        return got0[i, state:state + 1, :] * inc[g] + got0[i, :state, :]

    def lanes_of(d):
        return pl.ds(pl.multiple_of(peer(d) * CHUNK, CHUNK), CHUNK)

    @pl.when(ahead)
    def _():
        for d in range(groups):
            hst[:, lanes_of(d)] = own(d)

    @pl.when(behind)
    def _():
        for d in range(groups):
            hand(peer(d)).wait_recv()
            hst[:, lanes_of(d)] = fin[peer(d)]

    chunks = [slice(c * CHUNK, (c + 1) * CHUNK) for c in range(groups)]
    for c in chunks:
        h = hst[:, c] * rows[blocks:blocks + 1, c]
        hst[:, c] = h
        hz[0, :128, c], hz[0, 128:, c] = halves(h)

    @pl.loop(0, blocks)
    def _(k):
        span = pl.ds(pl.multiple_of(k * Q, Q), Q)
        now = lax.rem(k, 2)
        first, second = abuf[k, :192], abuf[k, 192:]
        come = blocks + jnp.minimum(k + 1, blocks - 1)
        for c in chunks:
            wide = xbuf[k, :, c]
            one = dot_nn(first, jnp.concatenate([hz[now, :128, c], wide], axis=0))
            two = dot_nn(second, jnp.concatenate([wide, hz[now, 128:, c]], axis=0))
            lifted = lbuf[k, 64:, c].astype(F32) + lbuf[k, :64, c].astype(F32)
            bt[0:64, c], bt[64:128, c] = halves(lifted * (one[:64] + two))
            h = (hst[:, c] + one[64:]) * rows[pl.ds(k, 1), c]
            h = h * jnp.where(k == blocks - 1, 1.0, rows[pl.ds(come, 1), c])
            hst[:, c] = h
            hz[1 - now, :128, c], hz[1 - now, 128:, c] = halves(h)
        sums = dot_nt(bt[...], sel[...])
        vs[span, :] = sums[0:64] + sums[64:128]
        r = dot_nt(hz[now], lbuf[k])
        turned = jnp.transpose(r[:128] + r[128:])
        grad_c = part[span, LANES:] + turned[:64] + turned[64:]
        part[span, LANES:] = grad_c

        @pl.when(k < early)
        def _():
            total_c.send(k, grad_c)

        @pl.when((k >= LAG) & (k < early + LAG))
        def _():
            total_c.reduce(k - LAG)

        @pl.when(k >= 2 * LAG)
        def _():
            j = k - 2 * LAG
            part[pl.ds(pl.multiple_of(j * Q, Q), Q), LANES:] = total_c.result(j)

        @pl.when((k == blocks // 4) & behind)
        def _():
            scan()

        @pl.when((k == 3 * blocks // 4) & behind)
        def _():
            hand_all()

    @pl.when(ahead)
    def _():
        for d in range(groups):
            hand(peer(d)).wait_recv()
            gin_ref[peer(d)] = fin[peer(d)]

    @pl.when(behind)
    def _():
        for d in range(groups):
            gin_ref[peer(d)] = own(d)

    for i in range(groups):
        swap(i).wait_send()
        hand(i).wait_send()
    for d in range(1, groups):
        spread(d).wait_send()
        back(peer(d)).wait_send()
    for i in range(groups):
        for copy in puts(i):
            copy.wait()
    put_ab.wait()
    total_c.sent()


def edges(x, y, bc, dt, bias, alog, skip):
    length, width = x.shape
    heads = dt.shape[0]
    state = bc.shape[1] // 2
    groups = width // CHUNK
    blocks = length // Q
    whole = pl.BlockSpec(memory_space=pltpu.VMEM)
    anywhere = pl.BlockSpec(memory_space=pl.ANY)
    dma = pltpu.SemaphoreType.DMA
    return pl.pallas_call(
        functools.partial(edges_kernel, heads),
        out_shape=(
            jax.ShapeDtypeStruct((groups, state, CHUNK), F32),
            jax.ShapeDtypeStruct((state, width), F32),
            jax.ShapeDtypeStruct((8, LANES), F32),
            jax.ShapeDtypeStruct((length, 2 * state), F32),
            jax.ShapeDtypeStruct((length, LANES), F32),
            jax.ShapeDtypeStruct((length, LANES), F32),
            jax.ShapeDtypeStruct((2 * blocks + 8, width), F32),
            jax.ShapeDtypeStruct((length, LANES), F32),
            jax.ShapeDtypeStruct((blocks, 2 * Q, width), BF16),
            jax.ShapeDtypeStruct((blocks, 2 * Q, width), BF16),
            jax.ShapeDtypeStruct((length, width), F32),
            jax.ShapeDtypeStruct((blocks, 4 * Q, 4 * Q), BF16),
        ),
        in_specs=[anywhere, anywhere] + [whole] * 5,
        out_specs=(whole,) * 8 + (anywhere,) * 4,
        scratch_shapes=[
            pltpu.VMEM((length, LANES), BF16),
            pltpu.VMEM((length, LANES), BF16),
            pltpu.VMEM((length, LANES), BF16),
            pltpu.VMEM((length, LANES), BF16),
            pltpu.VMEM((state, 2 * length), BF16),
            pltpu.VMEM((state, 2 * length), BF16),
            pltpu.VMEM((LANES, width), BF16),
            pltpu.VMEM((groups, length, CHUNK), BF16),
            pltpu.VMEM((groups, length, CHUNK), BF16),
            pltpu.VMEM((2 * length, CHUNK), BF16),
            pltpu.VMEM((8, LANES), BF16),
            pltpu.VMEM((groups, state + 8, CHUNK), F32),
            pltpu.VMEM((groups, state + 8, CHUNK), F32),
            pltpu.VMEM((groups - 1, state + 8, CHUNK), F32),
            pltpu.VMEM((groups, state + 8, CHUNK), F32),
            pltpu.VMEM((groups, state, CHUNK), F32),
            pltpu.VMEM((groups, state, CHUNK), F32),
            pltpu.VMEM((groups, state, CHUNK), F32),
            pltpu.VMEM((blocks, 2 * Q, width), BF16),
            pltpu.VMEM((blocks, 2 * Q, width), BF16),
            pltpu.VMEM((length, width), F32),
            pltpu.VMEM((blocks, 4 * Q, 4 * Q), BF16),
            pltpu.VMEM((blocks, 4 * Q, 4 * Q), BF16),
            pltpu.VMEM((8, width), F32),
            pltpu.VMEM((2, 256, width), BF16),
            dma((2, groups)),
            dma((groups,)), dma((groups,)),
            dma((groups,)), dma((groups,)),
            dma((groups,)), dma((groups,)),
            dma((groups,)), dma((groups,)),
            dma((3, groups)), dma,
        ] + head_sum_scratch(blocks - 2 * LAG, lax.axis_size("head")),
        compiler_params=pltpu.CompilerParams(vmem_limit_bytes=VMEM_LIMIT, collective_id=0, has_side_effects=True),
        cost_estimate=pl.CostEstimate(flops=8 * length * width * state, bytes_accessed=4 * length * width, transcendentals=0),
    )(x, y, bc, dt, bias, alog, skip)


def main_kernel(heads, zs, dps, flats, scale, xb_ref, lb_ref, fb_ref, yb_ref, ab_ref,
                gin_ref, hend_ref, dskip_ref, part_ref, dts, shs, rows, vs, alog_ref,
                gx_ref, gbc_ref, gdt_ref, gheads_ref,
                sel, gdts, gz, prods, gst, carry, hsum, hgot, hmid, hall, s3, r3, s4, r4,
                b_stage, b_landed, b_done, b1, b2, b3, b4, c_stage, c_landed, c_done, c1, c2, c3, c4):
    length = dts.shape[0]
    width = sel.shape[1]
    blocks = length // Q
    step = pl.program_id(0)
    kb = blocks - 1 - step
    chunks = [slice(c * CHUNK, (c + 1) * CHUNK) for c in range(width // CHUNK)]
    rate = rates_of(alog_ref, heads)
    total_b = HeadSum(b_stage, b_landed, b_done, (b1, b2, b3, b4))
    total_c = HeadSum(c_stage, c_landed, c_done, (c1, c2, c3, c4))
    late = c_stage.shape[0]
    flat = lax.axis_index("seq") * dps + lax.axis_index("dp")
    near = hgot.shape[0]
    far = hall.shape[0]
    inner, outer = lax.rem(flat, near), flat // near
    barrier = pltpu.get_barrier_semaphore()

    def at(flat):
        return {"seq": flat // dps, "dp": lax.rem(flat, dps)}

    def share(d, source):
        return pltpu.make_async_remote_copy(
            src_ref=hsum, dst_ref=hgot.at[source], send_sem=s3.at[d], recv_sem=r3.at[source],
            device_id=at(outer * near + lax.rem(inner + d, near)), device_id_type=pl.DeviceIdType.MESH)

    def spread(d, source):
        return pltpu.make_async_remote_copy(
            src_ref=hmid, dst_ref=hall.at[source], send_sem=s4.at[d], recv_sem=r4.at[source],
            device_id=at(lax.rem(outer + d, far) * near + inner), device_id_type=pl.DeviceIdType.MESH)

    def rows_of(k):
        return pl.ds(pl.multiple_of(k * Q, Q), Q)

    @pl.when(step == 0)
    def _():
        greet_heads(barrier, zs)
        for d in range(1, near):
            pl.semaphore_signal(barrier, inc=1, device_id=at(outer * near + lax.rem(inner + d, near)),
                                device_id_type=pl.DeviceIdType.MESH)
        for d in range(1, far):
            pl.semaphore_signal(barrier, inc=1, device_id=at(lax.rem(outer + d, far) * near + inner),
                                device_id_type=pl.DeviceIdType.MESH)
        sel[...] = head_lanes(heads, width)
        for i, c in enumerate(chunks):
            g = gin_ref[i] * rows[blocks - 1:blocks, c]
            gst[:, c] = g
            gz[0, :128, c], gz[0, 128:, c] = halves(g)
        closing = jnp.concatenate(
            [jnp.sum(gin_ref[i] * hend_ref[:, c], axis=0, keepdims=True) for i, c in enumerate(chunks)], axis=1)
        hi, lo = halves(jnp.broadcast_to(closing, (16, width)))
        carry[...] = (dot_nt(hi, sel[...]) + dot_nt(lo, sel[...]))[:8]
        hsum[...] = jnp.where(iota(hsum.shape, 0) == 2, dskip_ref[...], 0.0)
        gbc_ref[:(blocks - late) * Q, LANES:] = part_ref[:(blocks - late) * Q, LANES:]

    span = pl.ds(pl.multiple_of(kb * Q, Q), Q)
    now = lax.rem(step, 2)
    first, second = ab_ref[0, :192], ab_ref[0, 192:]
    come = jnp.maximum(kb - 1, 0)
    for c in chunks:
        wide = lb_ref[0, :, c]
        one = dot_nn(first, jnp.concatenate([gz[now, :128, c], wide], axis=0))
        two = dot_nn(second, jnp.concatenate([wide, gz[now, 128:, c]], axis=0))
        out = one[:64] + two
        xs = xb_ref[0, 64:, c].astype(F32) + xb_ref[0, :64, c].astype(F32)
        prods[0:64, c], prods[64:128, c] = halves(xs * out)
        gx_ref[:, c] = (fb_ref[:, c] * out + rows[2 * blocks:2 * blocks + 1, c] * yb_ref[:, c].astype(F32)).astype(BF16)
        g = (gst[:, c] + one[64:]) * rows[pl.ds(blocks + kb, 1), c] * rows[pl.ds(come, 1), c]
        gst[:, c] = g
        gz[1 - now, :128, c], gz[1 - now, 128:, c] = halves(g)

    sums = dot_nt(prods[...], sel[...])
    w = sums[0:64] + sums[64:128]
    dt = dts[span, :]
    dlog = dot_nn(triangle(True), vs[span, :] - w, HIGH) + carry[0:1]
    carry[...] = jnp.broadcast_to(dlog[0:1], carry.shape)
    grad_dt = (w / dt + dlog * rate) * jax.nn.sigmoid(shs[span, :])
    gdts[span, :] = grad_dt
    hsum[0:1] += jnp.sum(dlog * dt, axis=0, keepdims=True) * rate
    hsum[1:2] += jnp.sum(grad_dt, axis=0, keepdims=True)
    r = dot_nt(gz[now], xb_ref[0])
    turned = jnp.transpose(r[:128] + r[128:])

    @pl.when(step == 0)
    def _():
        pl.semaphore_wait(barrier, zs - 1 + near - 1 + far - 1)

    total_b.send(step, part_ref[span, :LANES] + turned[:64] + turned[64:])

    @pl.when(step < late)
    def _():
        total_c.send(step, part_ref[span, LANES:])

    def reduce(j):
        total_b.reduce(j)

        @pl.when(j < late)
        def _():
            total_c.reduce(j)

    def finish(j):
        gbc_ref[rows_of(blocks - 1 - j), :LANES] = total_b.result(j)

        @pl.when(j < late)
        def _():
            gbc_ref[rows_of(blocks - 1 - j), LANES:] = total_c.result(j)

    @pl.when(step >= LAG)
    def _():
        reduce(step - LAG)

    @pl.when(step >= 2 * LAG)
    def _():
        finish(step - 2 * LAG)

    @pl.when(step == blocks - 1)
    def _():
        for d in range(1, near):
            share(d, inner).start()
        hgot[inner] = hsum[...]
        for j in range(blocks - LAG, blocks):
            total_b.reduce(j)
        gdt_ref[...] = jnp.transpose(gdts[...])[:heads]
        for d in range(1, near):
            share(d, lax.rem(inner + d, near)).wait_recv()
        total = hgot[0]
        for other in range(1, near):
            total = total + hgot[other]
        hmid[...] = total
        hall[outer] = total
        for d in range(1, far):
            spread(d, outer).start()
        for j in range(blocks - 2 * LAG, blocks):
            gbc_ref[rows_of(blocks - 1 - j), :LANES] = total_b.result(j)
        for d in range(1, far):
            spread(d, lax.rem(outer + d, far)).wait_recv()
        total = hall[0]
        for other in range(1, far):
            total = total + hall[other]
        gheads_ref[...] = total[:3, :heads] * scale
        for d in range(1, near):
            share(d, inner).wait_send()
        for d in range(1, far):
            spread(d, outer).wait_send()
        total_b.sent()
        total_c.sent()


def main(heads, y, alog, gin, hend, dskip, part, dts, shs, rows, vs, xs, ls, fs, ab):
    length, width = y.shape
    state = gin.shape[1]
    blocks = length // Q
    zs, dps = lax.axis_size("head"), lax.axis_size("dp")
    flats = lax.axis_size("seq") * dps
    scale = 1.0 / math.sqrt(flats * length)
    near = math.gcd(flats, 8)
    dma = pltpu.SemaphoreType.DMA
    whole = pl.BlockSpec(memory_space=pltpu.VMEM)
    back = pl.BlockSpec((Q, width), lambda i: (blocks - 1 - i, 0))
    pair_b = pl.BlockSpec((1, 2 * Q, width), lambda i: (blocks - 1 - i, 0, 0))
    left_b = pl.BlockSpec((1, 4 * Q, 4 * Q), lambda i: (blocks - 1 - i, 0, 0))
    return pl.pallas_call(
        functools.partial(main_kernel, heads, zs, dps, flats, scale),
        grid=(blocks,),
        out_shape=(
            jax.ShapeDtypeStruct((length, width), BF16),
            jax.ShapeDtypeStruct((length, 2 * state), F32),
            jax.ShapeDtypeStruct((heads, length), F32),
            jax.ShapeDtypeStruct((3, heads), F32),
        ),
        in_specs=[pair_b, pair_b, back, back, left_b] + [whole] * 9,
        out_specs=(back, whole, whole, whole),
        scratch_shapes=[
            pltpu.VMEM((LANES, width), BF16),
            pltpu.VMEM((length, LANES), F32),
            pltpu.VMEM((2, 256, width), BF16),
            pltpu.VMEM((128, width), BF16),
            pltpu.VMEM((state, width), F32),
            pltpu.VMEM((8, LANES), F32),
            pltpu.VMEM((8, LANES), F32),
            pltpu.VMEM((near, 8, LANES), F32),
            pltpu.VMEM((8, LANES), F32),
            pltpu.VMEM((flats // near, 8, LANES), F32),
            dma((near,)), dma((near,)), dma((flats // near,)), dma((flats // near,)),
        ] + head_sum_scratch(blocks, zs) + head_sum_scratch(2 * LAG, zs),
        compiler_params=pltpu.CompilerParams(
            vmem_limit_bytes=VMEM_LIMIT, collective_id=1, has_side_effects=True, dimension_semantics=("arbitrary",)),
        cost_estimate=pl.CostEstimate(flops=60 * length * width * state, bytes_accessed=12 * length * width, transcendentals=0),
    )(xs, ls, fs, y, ab, gin, hend, dskip, part, dts, shs, rows, vs, alog)


def shards(inputs_x, inputs_bc, dt_raw, grad_out, a_log, dt_bias, skip):
    heads = a_log.shape[0]
    x, y, bc, dt = inputs_x[0], grad_out[0], inputs_bc[0], dt_raw[0].T
    bias, alog, skips = dt_bias[None], a_log[None], skip[None]
    prepared = edges(x, y, bc, dt, bias, alog, skips)
    grad_x, grad_bc, grad_dt, sums = main(heads, y, alog, *prepared)
    return (grad_x[None], grad_bc[None], grad_dt.T[None], sums)


def solution(mesh):
    placed = (
        P("dp", "seq", "head"),
        P("dp", "seq", None),
        P("dp", "seq", "head"),
        P("dp", "seq", "head"),
        P("head"),
        P("head"),
        P("head"),
    )
    return jax.shard_map(
        shards,
        mesh=mesh,
        in_specs=placed,
        out_specs=(
            P("dp", "seq", "head"),
            P("dp", "seq", None),
            P("dp", "seq", "head"),
            P(None, "head"),
        ),
        check_vma=False,
    )
```

```python
import functools
import math

import jax
import jax.numpy as jnp
from jax import lax
from jax.experimental import pallas as pl
from jax.experimental.pallas import tpu as pltpu
from jax.sharding import PartitionSpec as P

Q = 64
LAG = 4
CHUNK = 256
HEADDIM = 64
LANES = 128
HIGH = lax.Precision.HIGHEST
F32 = jnp.float32
BF16 = jnp.bfloat16
VMEM_LIMIT = 60 * 1024 * 1024


def dot_nn(a, b, precision=None):
    return lax.dot_general(a, b, (((1,), (0,)), ((), ())), precision=precision, preferred_element_type=F32)


def dot_nt(a, b):
    return lax.dot_general(a, b, (((1,), (1,)), ((), ())), preferred_element_type=F32)


def halves(value):
    hi = value.astype(BF16)
    return hi, (value - hi.astype(F32)).astype(BF16)


def iota(shape, dim):
    return lax.broadcasted_iota(jnp.int32, shape, dim)


def triangle(upper):
    r, c = iota((Q, Q), 0), iota((Q, Q), 1)
    return jnp.where(r <= c if upper else r >= c, 1.0, 0.0).astype(F32)


def repeat_heads(value, heads):
    pick = jnp.where(iota((heads, LANES), 1) % heads == iota((heads, LANES), 0), 1.0, 0.0)
    return dot_nn(value, pick.astype(F32), HIGH)


def packed(value, heads, terms):
    lane = iota(value.shape, 1)
    total = jnp.zeros_like(value)
    rest = value
    for term in range(terms):
        part = rest.astype(BF16).astype(F32)
        total = jnp.where((lane >= term * heads) & (lane < (term + 1) * heads), part, total)
        rest = rest - part
    return total.astype(BF16)


def head_lanes(heads, width):
    shape = (LANES, width)
    return jnp.where(iota(shape, 0) % heads == iota(shape, 1) // HEADDIM, 1.0, 0.0).astype(BF16)


def steps_of(dt_ref, bias_ref, heads):
    turned = jnp.transpose(jnp.concatenate([dt_ref[...]] * (LANES // heads), axis=0))
    return turned + repeat_heads(jnp.broadcast_to(bias_ref[...], (8, heads)), heads)[:1]


def rates_of(alog_ref, heads):
    return -jnp.exp(repeat_heads(jnp.broadcast_to(alog_ref[...], (8, heads)), heads))[:1]


class HeadSum:
    def __init__(self, stage, landed, done, sems):
        self.stage, self.landed, self.done = stage, landed, done
        self.s1, self.r1, self.s2, self.r2 = sems
        self.zs, self.z = stage.shape[1], lax.axis_index("head")

    def peer(self, d):
        return lax.rem(self.z + d, self.zs)

    def copy(self, src, dst, send, recv, q):
        return pltpu.make_async_remote_copy(
            src_ref=src, dst_ref=dst, send_sem=send, recv_sem=recv,
            device_id={"head": q}, device_id_type=pl.DeviceIdType.MESH)

    def scatter(self, j, d):
        q = self.peer(d)
        return self.copy(self.stage.at[j, q], self.landed.at[j, self.z], self.s1.at[j, q], self.r1.at[j, self.z], q)

    def gather(self, j, d):
        q = self.peer(d)
        return self.copy(self.done.at[j, self.z], self.done.at[j, self.z], self.s2.at[j, q], self.r2.at[j, self.z], q)

    def send(self, j, value):
        self.stage[j] = value.reshape(self.stage.shape[1:])
        for d in range(1, self.zs):
            self.scatter(j, d).start()

    def reduce(self, j):
        for d in range(1, self.zs):
            q = self.peer(d)
            self.copy(self.stage.at[j, q], self.landed.at[j, q], self.s1.at[j, q], self.r1.at[j, q], q).wait_recv()
        self.landed[j, self.z] = self.stage[j, self.z]
        total = self.landed[j, 0]
        for q in range(1, self.zs):
            total = total + self.landed[j, q]
        self.done[j, self.z] = total
        for d in range(1, self.zs):
            self.gather(j, d).start()

    def result(self, j):
        for d in range(1, self.zs):
            q = self.peer(d)
            self.copy(self.done.at[j, q], self.done.at[j, q], self.s2.at[j, q], self.r2.at[j, q], q).wait_recv()
        return self.done[j].reshape(-1, LANES)

    def sent(self):
        @pl.loop(0, self.stage.shape[0])
        def _(j):
            for d in range(1, self.zs):
                self.scatter(j, d).wait_send()
                self.gather(j, d).wait_send()


def head_sum_scratch(count, zs, lines):
    buffer = pltpu.VMEM((count, zs, lines, LANES), F32)
    return [buffer] * 3 + [pltpu.SemaphoreType.DMA((count, zs))] * 4


def greet_heads(barrier, zs):
    for d in range(1, zs):
        pl.semaphore_signal(barrier, inc=1, device_id={"head": lax.rem(lax.axis_index("head") + d, zs)},
                            device_id_type=pl.DeviceIdType.MESH)


def edges_kernel(heads, x_ref, y_ref, bc_ref, dt_ref, bias_ref, alog_ref, weight_ref,
                 gin_ref, hst, skip_ref, part, dts, shs, rows, vs, xo_ref, lo_ref, fo_ref, ab_ref,
                 pe, pf, le, lf, bt, ct, sel, xb, yb, xs, dec, out0, got0, chip, gath, pre, inc, fin,
                 xbuf, lbuf, fbuf, abuf, bbuf, yx, hz,
                 load_sem, s0, r0, s1, r1, s2, r2, s3, r3, put_sem, put_one):
    length = bc_ref.shape[0]
    blocks = length // Q
    groups = gin_ref.shape[0]
    state = gin_ref.shape[1]
    me = lax.axis_index("seq")
    core = lax.rem(me, 2)
    place = me // 2
    ahead = core == 1
    behind = core == 0
    partner = me + 1 - 2 * core

    def peer(d):
        return lax.rem(place + d, groups)

    def loads(i):
        g = peer(1 + i)
        span = pl.ds(pl.multiple_of(g * CHUNK, CHUNK), CHUNK)
        return (pltpu.make_async_copy(x_ref.at[:, span], xb.at[i], load_sem.at[0, i]),
                pltpu.make_async_copy(y_ref.at[:, span], yb.at[i], load_sem.at[1, i]))

    def swap(i):
        return pltpu.make_async_remote_copy(
            src_ref=out0.at[i], dst_ref=got0.at[i], send_sem=s0.at[i], recv_sem=r0.at[i],
            device_id={"seq": partner}, device_id_type=pl.DeviceIdType.MESH)

    def spread(d):
        return pltpu.make_async_remote_copy(
            src_ref=chip.at[d - 1], dst_ref=gath.at[place], send_sem=s1.at[d - 1], recv_sem=r1.at[place],
            device_id={"seq": peer(d) * 2 + core}, device_id_type=pl.DeviceIdType.MESH)

    def spread_in(source):
        return pltpu.make_async_remote_copy(
            src_ref=chip.at[0], dst_ref=gath.at[source], send_sem=s1.at[0], recv_sem=r1.at[source],
            device_id={"seq": source * 2 + core}, device_id_type=pl.DeviceIdType.MESH)

    def back(pos):
        return pltpu.make_async_remote_copy(
            src_ref=pre.at[pos], dst_ref=inc.at[place], send_sem=s2.at[pos], recv_sem=r2.at[place],
            device_id={"seq": pos * 2 + core}, device_id_type=pl.DeviceIdType.MESH)

    def back_in(source):
        return pltpu.make_async_remote_copy(
            src_ref=pre.at[source], dst_ref=inc.at[source], send_sem=s2.at[source], recv_sem=r2.at[source],
            device_id={"seq": source * 2 + core}, device_id_type=pl.DeviceIdType.MESH)

    def hand(g):
        return pltpu.make_async_remote_copy(
            src_ref=inc.at[g], dst_ref=fin.at[g], send_sem=s3.at[g], recv_sem=r3.at[g],
            device_id={"seq": partner}, device_id_type=pl.DeviceIdType.MESH)

    for i in range(groups):
        for copy in loads(i):
            copy.start()
    barrier = pltpu.get_barrier_semaphore()
    pl.semaphore_signal(barrier, inc=1, device_id={"seq": partner}, device_id_type=pl.DeviceIdType.MESH)
    for d in range(1, groups):
        pl.semaphore_signal(barrier, inc=1, device_id={"seq": peer(d) * 2 + core}, device_id_type=pl.DeviceIdType.MESH)

    sel[...] = head_lanes(heads, sel.shape[1])
    rate = rates_of(alog_ref, heads)
    shifted = steps_of(dt_ref, bias_ref, heads)
    shs[...] = shifted
    dt = jax.nn.softplus(shifted)
    dts[...] = dt
    tri = triangle(False)
    cums = [dot_nn(tri, dt[k * Q:(k + 1) * Q] * rate, HIGH) for k in range(blocks)]
    before = jnp.zeros((1, LANES), F32)
    for k in range(blocks):
        mid = cums[k][Q // 2 - 1:Q // 2]
        le[pl.ds(k * Q, Q), :] = packed(jnp.exp(cums[k] - mid), heads, 2)
        lf[pl.ds(k * Q, Q), :] = packed(dt[k * Q:(k + 1) * Q] * jnp.exp(mid - cums[k]), heads, 2)
        pe[pl.ds(k * Q, Q), :] = packed(jnp.exp(cums[k] + before), heads, 2)
        before = before + cums[k][Q - 1:Q]
    after = jnp.zeros((1, LANES), F32)
    for k in reversed(range(blocks)):
        last = cums[k][Q - 1:Q]
        pf[pl.ds(k * Q, Q), :] = packed(dt[k * Q:(k + 1) * Q] * jnp.exp((last - cums[k]) + after), heads, 2)
        after = after + last
    dec[...] = packed(jnp.broadcast_to(jnp.exp(before), (8, LANES)), heads, 3)
    b_t = jnp.transpose(bc_ref[:, :LANES].astype(F32)).astype(BF16)
    c_t = jnp.transpose(bc_ref[:, LANES:].astype(F32)).astype(BF16)
    bt[:, :length] = b_t
    bt[:, length:] = b_t
    ct[:, :length] = c_t
    ct[:, length:] = c_t
    pl.semaphore_wait(barrier, groups)

    def combine(i):
        swap(i).wait_recv()
        keep = out0[i, state:state + 1, :]
        value = pre[i] + keep * got0[i, :state, :]
        decay = out0[i, state:, :] * got0[i, state:, :]
        if i < groups - 1:
            chip[i, :state, :] = value
            chip[i, state:, :] = decay

            @pl.when(ahead)
            def _():
                spread(i + 1).start()
        else:
            gath[place, :state, :] = value
            gath[place, state:, :] = decay

    for i in range(groups):
        g = peer(1 + i)
        here = sel[:, pl.ds(pl.multiple_of(g * CHUNK, CHUNK), CHUNK)]
        copy_x, copy_y = loads(i)
        copy_x.wait()
        hi, lo = halves(dot_nn(pf[...], here) * xb[i].astype(F32))
        xs[:length] = hi
        xs[length:] = lo
        ends = dot_nn(bt[...], xs[...])
        copy_y.wait()
        hi, lo = halves(dot_nn(pe[...], here) * yb[i].astype(F32))
        xs[:length] = hi
        xs[length:] = lo
        starts = dot_nn(ct[...], xs[...])
        pre[i] = jnp.where(ahead, ends, starts)
        out0[i, :state, :] = jnp.where(ahead, starts, ends)
        out0[i, state:, :] = dot_nn(dec[...], here)
        swap(i).start()
        if i:
            combine(i - 1)
    combine(groups - 1)

    def scan():
        total = jnp.zeros((state, CHUNK), F32)
        for d in range(1, groups):
            spread_in(peer(d)).wait_recv()
        for k in range(groups):
            pos = jnp.where(ahead, k, groups - 1 - k)

            @pl.when(pos == place)
            def _():
                inc[place] = total

            @pl.when(pos != place)
            def _():
                pre[pos] = total
                back(pos).start()

            total = gath[pos, state:state + 1, :] * total + gath[pos, :state, :]

    def puts(i):
        g = peer(1 + i)
        span = pl.ds(pl.multiple_of(g * CHUNK, CHUNK), CHUNK)
        return (pltpu.make_async_copy(xbuf.at[:, :, span], xo_ref.at[:, :, span], put_sem.at[0, i]),
                pltpu.make_async_copy(lbuf.at[:, :, span], lo_ref.at[:, :, span], put_sem.at[1, i]),
                pltpu.make_async_copy(fbuf.at[:, span], fo_ref.at[:, span], put_sem.at[2, i]))

    for i in range(groups):
        g = peer(1 + i)
        span = pl.ds(pl.multiple_of(g * CHUNK, CHUNK), CHUNK)
        here = sel[:, span]
        x = xb[i].astype(F32)
        y = yb[i].astype(F32)
        f = dot_nn(lf[...], here)
        fbuf[:, span] = f
        hi, lo = halves(f * x)
        xbuf[:, :Q, span] = lo.reshape(blocks, Q, CHUNK)
        xbuf[:, Q:, span] = hi.reshape(blocks, Q, CHUNK)
        hi, lo = halves(dot_nn(le[...], here) * y)
        lbuf[:, :Q, span] = lo.reshape(blocks, Q, CHUNK)
        lbuf[:, Q:, span] = hi.reshape(blocks, Q, CHUNK)
        yx[:, span] = jnp.sum((y * x).reshape(length // 8, 8, CHUNK), axis=0)
        for copy in puts(i):
            copy.start()
        if i == groups // 2:
            pl.when(ahead)(scan)

    def hand_all():
        for d in range(groups):
            g = peer(d)
            if d:
                back_in(g).wait_recv()
            hand(g).start()

    def spread_all():
        for d in range(1, groups):
            spread(d).start()

    gone = jnp.concatenate([jnp.exp(cum[Q - 1:Q] - cum[Q // 2 - 1:Q // 2]) for cum in cums], axis=0)
    come = jnp.concatenate([jnp.exp(cum[Q // 2 - 1:Q // 2]) for cum in cums], axis=0)
    weights = repeat_heads(jnp.broadcast_to(weight_ref[...], (8, heads)), heads)
    rows[...] = dot_nn(packed(jnp.concatenate([gone, come, weights], axis=0), heads, 3), sel[...])

    lane = iota((Q, 2 * Q), 1)
    row = iota((Q, 2 * Q), 0)
    none = jnp.zeros((Q, 2 * Q), F32)

    @pl.loop(0, blocks)
    def _(k):
        span = pl.ds(pl.multiple_of(k * Q, Q), Q)
        b, c = bc_ref[span, :LANES], bc_ref[span, LANES:]
        bb = jnp.concatenate([b, b], axis=0)
        cc = jnp.concatenate([c, c], axis=0)
        lower = row >= lane % Q
        for dest, one, two, keep in ((abuf, c, bb, lower), (bbuf, b, cc, row <= lane % Q)):
            s_hi, s_lo = halves(jnp.where(keep, dot_nt(one, two), none))
            dest[k, :Q, :2 * Q] = one
            dest[k, :Q, 2 * Q:] = s_hi
            dest[k, Q:3 * Q, :2 * Q] = jnp.zeros((2 * Q, 2 * Q), BF16)
            dest[k, Q:3 * Q, 2 * Q:] = jnp.transpose(two.astype(F32)).astype(BF16)
            dest[k, 3 * Q:, :2 * Q] = s_lo
            dest[k, 3 * Q:, 2 * Q:] = one
        r = dot_nt(lbuf[k], xbuf[k])
        pair = jnp.where(lower, r[:Q] + r[Q:], none)
        p_hi, p_lo = halves(pair)
        part[span, LANES:] = dot_nn(p_hi, bb) + dot_nn(p_lo, bb)
        turned = jnp.transpose(pair)
        t_hi, t_lo = halves(turned[:Q] + turned[Q:])
        part[span, :LANES] = dot_nn(t_hi, c) + dot_nn(t_lo, c)

        @pl.when((k == blocks // 4) & behind)
        def _():
            spread_all()

        @pl.when((k == blocks // 2) & ahead)
        def _():
            hand_all()

    put_ab = pltpu.make_async_copy(bbuf, ab_ref, put_one)
    put_ab.start()
    sums = jnp.sum(yx[...], axis=0, keepdims=True)
    hi, lo = halves(jnp.broadcast_to(sums, yx.shape))
    skip_ref[...] = dot_nt(hi, sel[...]) + dot_nt(lo, sel[...])

    def own(d):
        g = peer(d)
        i = (d - 1) % groups
        return got0[i, state:state + 1, :] * inc[g] + got0[i, :state, :]

    def lanes_of(d):
        return pl.ds(pl.multiple_of(peer(d) * CHUNK, CHUNK), CHUNK)

    @pl.when(ahead)
    def _():
        for d in range(groups):
            hst[:, lanes_of(d)] = own(d)

    @pl.when(behind)
    def _():
        for d in range(groups):
            hand(peer(d)).wait_recv()
            hst[:, lanes_of(d)] = fin[peer(d)]

    chunks = [slice(c * CHUNK, (c + 1) * CHUNK) for c in range(groups)]
    for c in chunks:
        h = hst[:, c] * rows[blocks:blocks + 1, c]
        hst[:, c] = h
        hz[0, :128, c], hz[0, 128:, c] = halves(h)

    @pl.loop(0, blocks)
    def _(k):
        span = pl.ds(pl.multiple_of(k * Q, Q), Q)
        now = lax.rem(k, 2)
        first, second = abuf[k, :192], abuf[k, 192:]
        come = blocks + jnp.minimum(k + 1, blocks - 1)
        for c in chunks:
            wide = xbuf[k, :, c]
            one = dot_nn(first, jnp.concatenate([hz[now, :128, c], wide], axis=0))
            two = dot_nn(second, jnp.concatenate([wide, hz[now, 128:, c]], axis=0))
            lifted = lbuf[k, 64:, c].astype(F32) + lbuf[k, :64, c].astype(F32)
            bt[0:64, c], bt[64:128, c] = halves(lifted * (one[:64] + two))
            h = (hst[:, c] + one[64:]) * rows[pl.ds(k, 1), c]
            h = h * jnp.where(k == blocks - 1, 1.0, rows[pl.ds(come, 1), c])
            hst[:, c] = h
            hz[1 - now, :128, c], hz[1 - now, 128:, c] = halves(h)
        sums = dot_nt(bt[...], sel[...])
        vs[span, :] = sums[0:64] + sums[64:128]
        r = dot_nt(hz[now], lbuf[k])
        turned = jnp.transpose(r[:128] + r[128:])
        part[span, LANES:] += turned[:64] + turned[64:]

        @pl.when((k == blocks // 4) & behind)
        def _():
            scan()

        @pl.when((k == 3 * blocks // 4) & behind)
        def _():
            hand_all()

    @pl.when(ahead)
    def _():
        for d in range(groups):
            hand(peer(d)).wait_recv()
            gin_ref[peer(d)] = fin[peer(d)]

    @pl.when(behind)
    def _():
        for d in range(groups):
            gin_ref[peer(d)] = own(d)

    for i in range(groups):
        swap(i).wait_send()
        hand(i).wait_send()
    for d in range(1, groups):
        spread(d).wait_send()
        back(peer(d)).wait_send()
    for i in range(groups):
        for copy in puts(i):
            copy.wait()
    put_ab.wait()


def edges(x, y, bc, dt, bias, alog, skip):
    length, width = x.shape
    heads = dt.shape[0]
    state = bc.shape[1] // 2
    groups = width // CHUNK
    blocks = length // Q
    whole = pl.BlockSpec(memory_space=pltpu.VMEM)
    anywhere = pl.BlockSpec(memory_space=pl.ANY)
    dma = pltpu.SemaphoreType.DMA
    return pl.pallas_call(
        functools.partial(edges_kernel, heads),
        out_shape=(
            jax.ShapeDtypeStruct((groups, state, CHUNK), F32),
            jax.ShapeDtypeStruct((state, width), F32),
            jax.ShapeDtypeStruct((8, LANES), F32),
            jax.ShapeDtypeStruct((length, 2 * state), F32),
            jax.ShapeDtypeStruct((length, LANES), F32),
            jax.ShapeDtypeStruct((length, LANES), F32),
            jax.ShapeDtypeStruct((2 * blocks + 8, width), F32),
            jax.ShapeDtypeStruct((length, LANES), F32),
            jax.ShapeDtypeStruct((blocks, 2 * Q, width), BF16),
            jax.ShapeDtypeStruct((blocks, 2 * Q, width), BF16),
            jax.ShapeDtypeStruct((length, width), F32),
            jax.ShapeDtypeStruct((blocks, 4 * Q, 4 * Q), BF16),
        ),
        in_specs=[anywhere, anywhere] + [whole] * 5,
        out_specs=(whole,) * 8 + (anywhere,) * 4,
        scratch_shapes=[
            pltpu.VMEM((length, LANES), BF16),
            pltpu.VMEM((length, LANES), BF16),
            pltpu.VMEM((length, LANES), BF16),
            pltpu.VMEM((length, LANES), BF16),
            pltpu.VMEM((state, 2 * length), BF16),
            pltpu.VMEM((state, 2 * length), BF16),
            pltpu.VMEM((LANES, width), BF16),
            pltpu.VMEM((groups, length, CHUNK), BF16),
            pltpu.VMEM((groups, length, CHUNK), BF16),
            pltpu.VMEM((2 * length, CHUNK), BF16),
            pltpu.VMEM((8, LANES), BF16),
            pltpu.VMEM((groups, state + 8, CHUNK), F32),
            pltpu.VMEM((groups, state + 8, CHUNK), F32),
            pltpu.VMEM((groups - 1, state + 8, CHUNK), F32),
            pltpu.VMEM((groups, state + 8, CHUNK), F32),
            pltpu.VMEM((groups, state, CHUNK), F32),
            pltpu.VMEM((groups, state, CHUNK), F32),
            pltpu.VMEM((groups, state, CHUNK), F32),
            pltpu.VMEM((blocks, 2 * Q, width), BF16),
            pltpu.VMEM((blocks, 2 * Q, width), BF16),
            pltpu.VMEM((length, width), F32),
            pltpu.VMEM((blocks, 4 * Q, 4 * Q), BF16),
            pltpu.VMEM((blocks, 4 * Q, 4 * Q), BF16),
            pltpu.VMEM((8, width), F32),
            pltpu.VMEM((2, 256, width), BF16),
            dma((2, groups)),
            dma((groups,)), dma((groups,)),
            dma((groups,)), dma((groups,)),
            dma((groups,)), dma((groups,)),
            dma((groups,)), dma((groups,)),
            dma((3, groups)), dma,
        ],
        compiler_params=pltpu.CompilerParams(vmem_limit_bytes=VMEM_LIMIT, collective_id=0, has_side_effects=True),
        cost_estimate=pl.CostEstimate(flops=8 * length * width * state, bytes_accessed=4 * length * width, transcendentals=0),
    )(x, y, bc, dt, bias, alog, skip)


def main_kernel(heads, zs, dps, flats, scale, xb_ref, lb_ref, fb_ref, yb_ref, ab_ref,
                gin_ref, hend_ref, dskip_ref, part_ref, dts, shs, rows, vs, alog_ref,
                gx_ref, gbc_ref, gdt_ref, gheads_ref,
                sel, gdts, gz, prods, gst, carry, hsum, hgot, hmid, hall, s3, r3, s4, r4,
                b_stage, b_landed, b_done, b1, b2, b3, b4, c_stage, c_landed, c_done, c1, c2, c3, c4):
    length = dts.shape[0]
    width = sel.shape[1]
    blocks = length // Q
    step = pl.program_id(0)
    kb = blocks - 1 - step
    chunks = [slice(c * CHUNK, (c + 1) * CHUNK) for c in range(width // CHUNK)]
    rate = rates_of(alog_ref, heads)
    total_c = HeadSum(c_stage, c_landed, c_done, (c1, c2, c3, c4))
    z = lax.axis_index("head")
    flat = lax.axis_index("seq") * dps + lax.axis_index("dp")
    near = hgot.shape[0]
    far = hall.shape[0]
    inner, outer = lax.rem(flat, near), flat // near
    barrier = pltpu.get_barrier_semaphore()

    def at(flat):
        return {"seq": flat // dps, "dp": lax.rem(flat, dps)}

    def share(d, source):
        return pltpu.make_async_remote_copy(
            src_ref=hsum, dst_ref=hgot.at[source], send_sem=s3.at[d], recv_sem=r3.at[source],
            device_id=at(outer * near + lax.rem(inner + d, near)), device_id_type=pl.DeviceIdType.MESH)

    def spread(d, source):
        return pltpu.make_async_remote_copy(
            src_ref=hmid, dst_ref=hall.at[source], send_sem=s4.at[d], recv_sem=r4.at[source],
            device_id=at(lax.rem(outer + d, far) * near + inner), device_id_type=pl.DeviceIdType.MESH)

    def rows_of(k):
        return pl.ds(pl.multiple_of(k * Q, Q), Q)

    @pl.when(step == 0)
    def _():
        greet_heads(barrier, zs)
        for d in range(1, near):
            pl.semaphore_signal(barrier, inc=1, device_id=at(outer * near + lax.rem(inner + d, near)),
                                device_id_type=pl.DeviceIdType.MESH)
        for d in range(1, far):
            pl.semaphore_signal(barrier, inc=1, device_id=at(lax.rem(outer + d, far) * near + inner),
                                device_id_type=pl.DeviceIdType.MESH)
        sel[...] = head_lanes(heads, width)
        for i, c in enumerate(chunks):
            g = gin_ref[i] * rows[blocks - 1:blocks, c]
            gst[:, c] = g
            gz[0, :128, c], gz[0, 128:, c] = halves(g)
        closing = jnp.concatenate(
            [jnp.sum(gin_ref[i] * hend_ref[:, c], axis=0, keepdims=True) for i, c in enumerate(chunks)], axis=1)
        hi, lo = halves(jnp.broadcast_to(closing, (16, width)))
        carry[...] = (dot_nt(hi, sel[...]) + dot_nt(lo, sel[...]))[:8]
        hsum[...] = jnp.where(iota(hsum.shape, 0) == 2, dskip_ref[...], 0.0)

    span = pl.ds(pl.multiple_of(kb * Q, Q), Q)
    now = lax.rem(step, 2)
    first, second = ab_ref[0, :192], ab_ref[0, 192:]
    come = jnp.maximum(kb - 1, 0)
    for c in chunks:
        wide = lb_ref[0, :, c]
        one = dot_nn(first, jnp.concatenate([gz[now, :128, c], wide], axis=0))
        two = dot_nn(second, jnp.concatenate([wide, gz[now, 128:, c]], axis=0))
        out = one[:64] + two
        xs = xb_ref[0, 64:, c].astype(F32) + xb_ref[0, :64, c].astype(F32)
        prods[0:64, c], prods[64:128, c] = halves(xs * out)
        gx_ref[:, c] = (fb_ref[:, c] * out + rows[2 * blocks:2 * blocks + 1, c] * yb_ref[:, c].astype(F32)).astype(BF16)
        g = (gst[:, c] + one[64:]) * rows[pl.ds(blocks + kb, 1), c] * rows[pl.ds(come, 1), c]
        gst[:, c] = g
        gz[1 - now, :128, c], gz[1 - now, 128:, c] = halves(g)

    sums = dot_nt(prods[...], sel[...])
    w = sums[0:64] + sums[64:128]
    dt = dts[span, :]
    dlog = dot_nn(triangle(True), vs[span, :] - w, HIGH) + carry[0:1]
    carry[...] = jnp.broadcast_to(dlog[0:1], carry.shape)
    grad_dt = (w / dt + dlog * rate) * jax.nn.sigmoid(shs[span, :])
    gdts[span, :] = grad_dt
    hsum[0:1] += jnp.sum(dlog * dt, axis=0, keepdims=True) * rate
    hsum[1:2] += jnp.sum(grad_dt, axis=0, keepdims=True)
    r = dot_nt(gz[now], xb_ref[0])
    turned = jnp.transpose(r[:128] + r[128:])

    @pl.when(step == 0)
    def _():
        pl.semaphore_wait(barrier, zs - 1 + near - 1 + far - 1)

        total_c.send(0, part_ref[:, LANES:])

    def owner(t):
        return lax.rem(blocks - 1 - t, zs)

    def to_owner(t, source):
        j = t // zs
        return pltpu.make_async_remote_copy(
            src_ref=b_stage.at[t], dst_ref=b_landed.at[j, source], send_sem=b1.at[t], recv_sem=b2.at[j, source],
            device_id={"head": owner(t)}, device_id_type=pl.DeviceIdType.MESH)

    def from_owner(t, dest):
        return pltpu.make_async_remote_copy(
            src_ref=b_done.at[t], dst_ref=b_done.at[t], send_sem=b3.at[t, dest], recv_sem=b4.at[t],
            device_id={"head": dest}, device_id_type=pl.DeviceIdType.MESH)

    def reduce(t):
        @pl.when(owner(t) == z)
        def _():
            j = t // zs
            for d in range(1, zs):
                source = lax.rem(z + d, zs)
                pltpu.make_async_remote_copy(
                    src_ref=b_stage.at[t], dst_ref=b_landed.at[j, source], send_sem=b1.at[t],
                    recv_sem=b2.at[j, source], device_id={"head": source},
                    device_id_type=pl.DeviceIdType.MESH).wait_recv()
            b_landed[j, z] = b_stage[t]
            total = b_landed[j, 0]
            for other in range(1, zs):
                total = total + b_landed[j, other]
            b_done[t] = total
            for d in range(1, zs):
                from_owner(t, lax.rem(z + d, zs)).start()

    def finish(t):
        @pl.when(owner(t) != z)
        def _():
            from_owner(t, owner(t)).wait_recv()

        gbc_ref[rows_of(blocks - 1 - t), :LANES] = b_done[t]

    b_stage[step] = part_ref[span, :LANES] + turned[:64] + turned[64:]

    @pl.when(owner(step) != z)
    def _():
        to_owner(step, z).start()

    @pl.when(step == blocks // 2)
    def _():
        total_c.reduce(0)

    @pl.when(step >= LAG)
    def _():
        reduce(step - LAG)

    @pl.when(step >= 2 * LAG)
    def _():
        finish(step - 2 * LAG)

    @pl.when(step == blocks - 1)
    def _():
        for d in range(1, near):
            share(d, inner).start()
        hgot[inner] = hsum[...]
        for t in range(blocks - LAG, blocks):
            reduce(t)
        gdt_ref[...] = jnp.transpose(gdts[...])[:heads]
        for d in range(1, near):
            share(d, lax.rem(inner + d, near)).wait_recv()
        total = hgot[0]
        for other in range(1, near):
            total = total + hgot[other]
        hmid[...] = total
        hall[outer] = total
        for d in range(1, far):
            spread(d, outer).start()
        gbc_ref[:, LANES:] = total_c.result(0)
        for t in range(blocks - 2 * LAG, blocks):
            finish(t)
        for d in range(1, far):
            spread(d, lax.rem(outer + d, far)).wait_recv()
        total = hall[0]
        for other in range(1, far):
            total = total + hall[other]
        gheads_ref[...] = total[:3, :heads] * scale
        for d in range(1, near):
            share(d, inner).wait_send()
        for d in range(1, far):
            spread(d, outer).wait_send()
        total_c.sent()

        @pl.loop(0, blocks)
        def _(t):
            @pl.when(owner(t) != z)
            def _():
                to_owner(t, z).wait_send()

            @pl.when(owner(t) == z)
            def _():
                for d in range(1, zs):
                    from_owner(t, lax.rem(z + d, zs)).wait_send()


def main(heads, y, alog, gin, hend, dskip, part, dts, shs, rows, vs, xs, ls, fs, ab):
    length, width = y.shape
    state = gin.shape[1]
    blocks = length // Q
    zs, dps = lax.axis_size("head"), lax.axis_size("dp")
    flats = lax.axis_size("seq") * dps
    scale = 1.0 / math.sqrt(flats * length)
    near = math.gcd(flats, 8)
    dma = pltpu.SemaphoreType.DMA
    whole = pl.BlockSpec(memory_space=pltpu.VMEM)
    back = pl.BlockSpec((Q, width), lambda i: (blocks - 1 - i, 0))
    pair_b = pl.BlockSpec((1, 2 * Q, width), lambda i: (blocks - 1 - i, 0, 0))
    left_b = pl.BlockSpec((1, 4 * Q, 4 * Q), lambda i: (blocks - 1 - i, 0, 0))
    return pl.pallas_call(
        functools.partial(main_kernel, heads, zs, dps, flats, scale),
        grid=(blocks,),
        out_shape=(
            jax.ShapeDtypeStruct((length, width), BF16),
            jax.ShapeDtypeStruct((length, 2 * state), F32),
            jax.ShapeDtypeStruct((heads, length), F32),
            jax.ShapeDtypeStruct((3, heads), F32),
        ),
        in_specs=[pair_b, pair_b, back, back, left_b] + [whole] * 9,
        out_specs=(back, whole, whole, whole),
        scratch_shapes=[
            pltpu.VMEM((LANES, width), BF16),
            pltpu.VMEM((length, LANES), F32),
            pltpu.VMEM((2, 256, width), BF16),
            pltpu.VMEM((128, width), BF16),
            pltpu.VMEM((state, width), F32),
            pltpu.VMEM((8, LANES), F32),
            pltpu.VMEM((8, LANES), F32),
            pltpu.VMEM((near, 8, LANES), F32),
            pltpu.VMEM((8, LANES), F32),
            pltpu.VMEM((flats // near, 8, LANES), F32),
            dma((near,)), dma((near,)), dma((flats // near,)), dma((flats // near,)),
            pltpu.VMEM((blocks, Q, LANES), F32),
            pltpu.VMEM((blocks // zs, zs, Q, LANES), F32),
            pltpu.VMEM((blocks, Q, LANES), F32),
            dma((blocks,)), dma((blocks // zs, zs)), dma((blocks, zs)), dma((blocks,)),
        ] + head_sum_scratch(1, zs, length // zs),
        compiler_params=pltpu.CompilerParams(
            vmem_limit_bytes=VMEM_LIMIT, collective_id=1, has_side_effects=True, dimension_semantics=("arbitrary",)),
        cost_estimate=pl.CostEstimate(flops=60 * length * width * state, bytes_accessed=12 * length * width, transcendentals=0),
    )(xs, ls, fs, y, ab, gin, hend, dskip, part, dts, shs, rows, vs, alog)


def shards(inputs_x, inputs_bc, dt_raw, grad_out, a_log, dt_bias, skip):
    heads = a_log.shape[0]
    x, y, bc, dt = inputs_x[0], grad_out[0], inputs_bc[0], dt_raw[0].T
    bias, alog, skips = dt_bias[None], a_log[None], skip[None]
    prepared = edges(x, y, bc, dt, bias, alog, skips)
    grad_x, grad_bc, grad_dt, sums = main(heads, y, alog, *prepared)
    return (grad_x[None], grad_bc[None], grad_dt.T[None], sums)


def solution(mesh):
    placed = (
        P("dp", "seq", "head"),
        P("dp", "seq", None),
        P("dp", "seq", "head"),
        P("dp", "seq", "head"),
        P("head"),
        P("head"),
        P("head"),
    )
    return jax.shard_map(
        shards,
        mesh=mesh,
        in_specs=placed,
        out_specs=(
            P("dp", "seq", "head"),
            P("dp", "seq", None),
            P("dp", "seq", "head"),
            P(None, "head"),
        ),
        check_vma=False,
    )
```
